32 devices in a mesh: row: 4 (over x, core), col: 4 (over z), panel: 2 (over y).
Axes of the slice: x: 2, y: 2, z: 4, core: 2. Of those that a mesh axis runs over, the one named last changes fastest.
Arguments:
- velocity: bfloat16 [4608, 6, 1024], P(('row', 'col'), None, 'panel'), may hold values from -6 to 6
- panel_weight: float32 [1024], P('panel'), may hold values from -0.21875 to 0.21875
- panel_group: int32 [1024], P('panel'), may hold values from 0 to 3
- tile_map: int32 [4, 4], replicated, may hold values from 0 to 3
- group_gain: float32 [4, 4], replicated, may hold values from 0.25 to 1
Outputs:
- qtf: float32 [4608, 2, 4608], P(('row', 'panel'), None, 'col')
The draws below stay inside these ranges and needn't reach their ends.
All inputs are finite; a program needn't handle non-finite values.
Results may differ from the reference program's by a relative error of at most 0.0029.
Values may be sent and summed in bfloat16 or wider, within the bound.
No kernel may reach another device: no remote copies, remote signals or barrier semaphores. Data moves between devices by JAX's collectives and lax.ppermute only.
A program may use at most 64 MiB of HBM per device.

```python
import math
import jax
import jax.numpy as jnp
from jax import lax

GROUPS = 4
COLS = 4608
PANELS = 1024
N_ROW = 4
N_COL = 4


def with_ends(result, rng, smallest, high):
    dims = result.shape
    place = [jax.random.randint(jax.random.fold_in(rng, axis), (), 0, dims[axis]) for axis in range(len(dims))]
    result = result.at[tuple(place)].set(smallest)
    longest = dims.index(max(dims))
    place[longest] = (place[longest] + 1) % dims[longest]
    return result.at[tuple(place)].set(high)


def level_of(rng, shape, shards, smallest, largest):
    loudness, own = 1.0, jax.random.fold_in(rng, 6)
    for position, blocks in shards:
        heights = jnp.exp(jax.random.uniform(jax.random.fold_in(own, position), (blocks,), jnp.float32, smallest / len(shards), largest / len(shards)))
        loudness = loudness * jnp.repeat(heights, shape[position] // blocks).reshape([-1 if axis == position else 1 for axis in range(len(shape))])
    return loudness


def gaussian(stream_key, dims, spread, bound, cuts=(), dtype=jnp.bfloat16):
    result = spread * jax.random.normal(stream_key, dims, jnp.float32)
    if cuts:
        result = result * level_of(stream_key, dims, cuts, -0.22, 0.18)
    return jnp.clip(result, -bound, bound).astype(dtype)


def setup_inputs(seed: int = 0) -> dict:
    key_list = jax.random.split(jax.random.key(seed), 6)
    return {
        "velocity": gaussian(key_list[0], (COLS, 6, PANELS), 1.0, 6.0, ((0, 16), (2, 2))),
        "panel_weight": gaussian(key_list[1], (PANELS,), (3 * PANELS // 4) ** -0.5, 0.21875, ((0, 2),), jnp.float32),
        "panel_group": with_ends(jax.random.randint(key_list[2], (PANELS,), 0, GROUPS), jax.random.fold_in(key_list[2], 1), 0, GROUPS - 1).astype(jnp.int32),
        "tile_map": with_ends(jax.random.randint(key_list[3], (N_ROW, N_COL), 0, GROUPS), jax.random.fold_in(key_list[3], 1), 0, GROUPS - 1).astype(jnp.int32),
        "group_gain": jnp.clip(jnp.exp(jax.random.uniform(key_list[4], (GROUPS, GROUPS), jnp.float32, math.log(0.25), math.log(1.0))), 0.25, 1.0),
    }


def reference(velocity, panel_weight, panel_group, tile_map, group_gain):
    tile_width = COLS // N_ROW
    velocity_f32 = velocity.astype(jnp.float32)
    rows_out = []
    for row_tile in range(N_ROW):
        row_parts = []
        for col_tile in range(N_COL):
            region = tile_map[row_tile, col_tile]
            panel_scale = panel_weight * group_gain[panel_group, region]
            left_block = velocity_f32[row_tile * tile_width:(row_tile + 1) * tile_width]
            weighted = (left_block * panel_scale[None, None, :]).astype(jnp.bfloat16)
            weighted = lax.optimization_barrier(weighted).astype(jnp.float32)
            right_block = velocity_f32[col_tile * tile_width:(col_tile + 1) * tile_width]
            left_re = weighted[:, :3].reshape(tile_width, -1)
            left_im = weighted[:, 3:].reshape(tile_width, -1)
            right_re = right_block[:, :3].reshape(tile_width, -1)
            right_im = right_block[:, 3:].reshape(tile_width, -1)
            high = lax.Precision.HIGHEST
            gram_aa = jnp.dot(left_re, right_re.T, precision=high, preferred_element_type=jnp.float32)
            gram_ab = jnp.dot(left_re, right_im.T, precision=high, preferred_element_type=jnp.float32)
            gram_ba = jnp.dot(left_im, right_re.T, precision=high, preferred_element_type=jnp.float32)
            gram_bb = jnp.dot(left_im, right_im.T, precision=high, preferred_element_type=jnp.float32)
            tile_sign = 1.0 if row_tile <= col_tile else -1.0
            real_part = gram_aa + tile_sign * gram_bb
            imag_part = gram_ba - tile_sign * gram_ab
            row_parts.append(jnp.stack((real_part, imag_part), axis=1))
        rows_out.append(jnp.concatenate(row_parts, axis=2))
    return jnp.concatenate(rows_out, axis=0)
```

```python
import functools

import jax
import jax.numpy as jnp
import numpy as np
from jax import lax
from jax.experimental import pallas as pl
from jax.experimental.pallas import tpu as pltpu
from jax.sharding import PartitionSpec as P

LANES = 128
SENDS = ((2, 4), (3, 4), (4, 4), (5, 4), (6, 4))


def route(n):
    step = lambda r: -1 if r % 2 == 0 else 1
    behind = lambda j, d: j if d == 1 else n - 1 - j
    moves = {"own": (0, None, [])}
    holds = {"own": {(r, j): j for r in range(n) for j in range(n)}}

    def add(name, slot, source, pairs):
        moves[name] = (slot, source, pairs)
        holds[name] = {b: holds[source][a] for a, b in pairs}

    def hops(sign, keep):
        return [
            ((r, j), (r, j + sign * step(r)))
            for r in range(n)
            for j in range(n)
            if 0 <= j + sign * step(r) < n and keep(behind(j, sign * step(r)))
        ]

    for t in range(1, n):
        add(f"p{t}", t, "own" if t == 1 else f"p{t - 1}", hops(1, lambda b: b >= t - 1))
    for m in range(1, n):
        for t in range(1, m + 1):
            add(f"q{m}_{t}", m + t, "own" if t == 1 else f"q{m - 1}_{t - 1}", hops(-1, lambda b: b + 1 == m))
    rows = {}
    for name, held in holds.items():
        for device, plane in held.items():
            rows.setdefault(device, {})[plane] = (moves[name][0], name)
    cols = {}
    spreads = {}
    for name, held in holds.items():
        slot = moves[name][0]
        for c in range(n):
            if (c, c) not in held:
                continue
            cols.setdefault((c, c), {})[held[c, c]] = (slot, name)
            for v in range(1, n):
                parent = v & (v - 1)
                source = f"{name}_v{parent}" if parent else name
                late = slot + bin(v >> 1).count("1")
                spreads.setdefault(f"{name}_v{v}", (late, source, []))[2].append(((c ^ parent, c), (c ^ v, c)))
                cols.setdefault((c ^ v, c), {})[held[c, c]] = (late, f"{name}_v{v}")
    return moves, spreads, rows, cols


def share_out(n, rows, cols):
    half = n // 2
    slots = sorted({s for s, _ in SENDS})
    tasks, send_pairs, arrives = {}, [[] for _ in SENDS], {}
    for r in range(n):
        for j in range(n):
            for y in range(2):
                ready = sorted(
                    (max(rows[r, j][kr][0], cols[r, j][kc][0]), kr, kc) for kr in range(n) for kc in range(n)
                )
                left = [b for b in ready if b[1] // half != y]
                for index, (slot, cap) in enumerate(SENDS):
                    able = [b for b in left if b[0] <= slot]
                    if not able or (len(able) < min(cap, len(left)) and index < len(SENDS) - 1):
                        continue
                    for place, b in enumerate(able[:cap]):
                        left.remove(b)
                        tasks.setdefault((r, j, y, slot), []).append((b[1], b[2], 1 + index, place))
                        arrives[r, j, 1 - y, b[1], b[2]] = (index, place)
                    send_pairs[index].append((r, j, y))
                assert not left
                for b in ready:
                    if b[1] // half == y:
                        slot = min(s for s in slots if s >= b[0])
                        place = (b[1] - y * half) * n + b[2]
                        tasks.setdefault((r, j, y, slot), []).append((b[1], b[2], 0, place))
    return slots, tasks, send_pairs, arrives


def rate(w_ref, group_ref, gain_ref, region):
    groups = group_ref[...]
    gain = jnp.zeros(groups.shape, jnp.float32)
    for g in range(gain_ref.shape[0]):
        gain = gain + jnp.where(groups == g, gain_ref[g, region], jnp.float32(0.0))
    return w_ref[...] * gain


def fetch(index, sources, kept, target, sem, h, p, gap):
    def pull(source):
        for c in range(6):
            pltpu.make_async_copy(
                source.at[c], target.at[pl.ds((c // 3) * gap, h), pl.ds((c % 3) * p, p)], sem
            ).start()

    for i, source in enumerate(sources):

        @pl.when(index == i)
        def _():
            pull(source)

    @pl.when(index >= len(sources))
    def _():
        pull(kept.at[index - len(sources)])


def landed(sources, target, sem, h, p, gap):
    for c in range(6):
        pltpu.make_async_copy(
            sources[0].at[c], target.at[pl.ds((c // 3) * gap, h), pl.ds((c % 3) * p, p)], sem
        ).wait()


def pack(stage, real, imag, h):
    tail, quarter = h % LANES, h // 2
    full = h // LANES
    for part, value in ((0, real), (1, imag)):
        for k in range(full):
            stage[pl.ds((part * full + k) * h, h), :] = value[:, k * LANES:(k + 1) * LANES].astype(stage.dtype)
        for fold in range(2):
            lane = (2 * fold + part) * tail
            stage[pl.ds(2 * full * h, quarter), lane:lane + tail] = value[
                fold * quarter:(fold + 1) * quarter, full * LANES:
            ].astype(stage.dtype)


def multiply_blocks(
    first, base, keeps, sources, caps, h, p, gap, table, tile_map, gain_ref, w_ref, group_ref, *refs
):
    srcs = refs[:sources]
    refs = refs[sources:] if first else refs[sources + 2:]
    own, kept = refs[:2]
    outs = refs[2:2 + len(caps)]
    left, right, stage_own, stage_out, l_sem, r_sem, o_sem, k_sem = refs[2 + len(caps):]
    count = table[base]
    copies = table[keeps]

    def keep(t, carry):
        code = table[keeps + 1 + t]
        for i, source in enumerate(srcs):

            @pl.when((code & 63) == i)
            def _():
                pltpu.make_async_copy(source, kept.at[code >> 6], k_sem).start()

        return carry

    lax.fori_loop(0, copies, keep, 0)
    sign = table[2].astype(jnp.float32)
    scale = rate(w_ref, group_ref, gain_ref, tile_map[table[0], table[1]])

    def entry(t):
        code = table[base + 1 + t]
        return code & 63, (code >> 6) & 63, (code >> 12) & 15, code >> 16

    @pl.when(count > 0)
    def _():
        fetch(entry(0)[1], srcs, kept, right.at[0], r_sem.at[0], h, p, gap)

    def task(t, before):
        row, col, kind, place = entry(t)
        slot = lax.rem(t, 2)

        @pl.when(row != before)
        def _():
            fetch(row, srcs, kept, left, l_sem, h, p, h)
            landed(srcs, left, l_sem, h, p, h)
            for c in range(3):
                raw = left[:, c * p:(c + 1) * p].astype(jnp.float32)
                left[:, c * p:(c + 1) * p] = (raw * scale).astype(jnp.bfloat16)

        @pl.when(t + 1 < count)
        def _():
            fetch(entry(t + 1)[1], srcs, kept, right.at[1 - slot], r_sem.at[1 - slot], h, p, gap)

        landed(srcs, right.at[slot], r_sem.at[slot], h, p, gap)
        product = lax.dot_general(
            left[...], right[slot], (((1,), (1,)), ((), ())), preferred_element_type=jnp.float32
        )
        real = product[:h, :h] + sign * product[h:, gap:gap + h]
        imag = product[h:, :h] - sign * product[:h, gap:gap + h]

        @pl.when(kind == 0)
        def _():
            pack(stage_own, real, imag, h)
            copy = pltpu.make_async_copy(stage_own, own.at[place], o_sem)
            copy.start()
            copy.wait()

        for k, out in enumerate(outs):

            @pl.when(kind == k + 1)
            def _():
                pack(stage_out, real, imag, h)
                copy = pltpu.make_async_copy(stage_out, out.at[place], o_sem)
                copy.start()
                copy.wait()

        return row

    lax.fori_loop(0, count, task, jnp.int32(-1))

    def finish(t, carry):
        pltpu.make_async_copy(srcs[0], kept.at[0], k_sem).wait()
        return carry

    lax.fori_loop(0, copies, finish, 0)


def add_up(base, n, h, table, own, *refs):
    recvs = refs[:len(SENDS)]
    out, mine, theirs, real, imag, image, m_sem, t_sem, o_sem = refs[len(SENDS):]
    blocks = (n // 2) * n
    full, tail, quarter = h // LANES, h % LANES, h // 2
    wide = n * h // LANES

    def load(b, slot):
        pltpu.make_async_copy(own.at[b], mine.at[slot], m_sem.at[slot]).start()
        code = table[base + b]
        for k, recv in enumerate(recvs):

            @pl.when((code & 15) == k)
            def _():
                pltpu.make_async_copy(recv.at[code >> 4], theirs.at[slot], t_sem.at[slot]).start()

    def written(chunk, k):
        return pltpu.make_async_copy(
            image.at[chunk % 2, pl.ds(2 * k * h, 2 * h)].reshape(h, 2, LANES),
            out.at[pl.ds(chunk * h, h), :, pl.ds(k * LANES, LANES)],
            o_sem.at[chunk % 2],
        )

    load(0, 0)
    for b in range(blocks):
        slot, chunk, kc = b % 2, b // n, b % n
        if b + 1 < blocks:
            load(b + 1, 1 - slot)
        pltpu.make_async_copy(own.at[0], mine.at[slot], m_sem.at[slot]).wait()
        pltpu.make_async_copy(recvs[0].at[0], theirs.at[slot], t_sem.at[slot]).wait()
        for part, line in ((0, real), (1, imag)):
            for k in range(full):
                at = pl.ds((part * full + k) * h, h)
                line[:, kc * h + k * LANES:kc * h + (k + 1) * LANES] = mine[slot, at, :] + theirs[
                    slot, at, :
                ].astype(jnp.float32)
            at = pl.ds(2 * full * h, quarter)
            rest = mine[slot, at, :] + theirs[slot, at, :].astype(jnp.float32)
            for fold in range(2):
                lane = (2 * fold + part) * tail
                line[
                    fold * quarter:(fold + 1) * quarter, kc * h + full * LANES:(kc + 1) * h
                ] = rest[:, lane:lane + tail]
        if kc == n - 1:
            buf = chunk % 2
            for part, line in ((0, real), (1, imag)):
                for k in range(wide):
                    image[buf, pl.ds(2 * k * h + part, h, stride=2), :] = line[:, k * LANES:(k + 1) * LANES]
            for k in range(wide):
                written(chunk, k).start()
    for chunk in range(n // 2):
        for k in range(wide):
            written(chunk, k).wait()


def tiled(mesh, h, p):
    n = mesh.shape["col"]
    half = n // 2
    moves, spreads, rows, cols = route(n)
    slots, tasks, send_pairs, arrives = share_out(n, rows, cols)
    gap = -(-h // LANES) * LANES
    block = 2 * h * h // LANES

    event = lambda slot: min(s for s in slots if s >= slot)
    parts = lambda r, j, kr, kc: ((*rows[r, j][kr], kr), (*cols[r, j][kc], n + kc))
    names = {s: {"own"} for s in slots}
    keeps = {}
    for (r, j, y, s), items in tasks.items():
        for kr, kc, _, _ in items:
            for slot, name, place in parts(r, j, kr, kc):
                names[event(slot)].add(name)
                if event(slot) < s and name != "own":
                    keeps.setdefault((r, j, y, event(slot)), set()).add((name, place))
    names = {s: sorted(v) for s, v in names.items()}
    most = {s: max(len(v) for k, v in tasks.items() if k[3] == s) for s in slots}
    kept_most = {s: max([len(v) for k, v in keeps.items() if k[3] == s], default=0) for s in slots}
    bases, kept_bases, size = {}, {}, 3
    for s in slots:
        bases[s] = size
        kept_bases[s] = size + 1 + most[s]
        size += 2 + most[s] + kept_most[s]
    final = size
    size += half * n
    table = np.zeros((n, n, 2, size), np.int32)
    for r in range(n):
        for j in range(n):
            for y in range(2):
                line = table[r, j, y]
                line[:3] = r, j, 1 if r <= j else -1
                for s in slots:
                    items = sorted(tasks.get((r, j, y, s), []), key=lambda i: (rows[r, j][i[0]][0], i[0], -i[2], i[3]))
                    line[bases[s]] = len(items)
                    for t, (kr, kc, kind, place) in enumerate(items):
                        code = 0
                        for shift, (slot, name, where) in zip((0, 6), parts(r, j, kr, kc)):
                            near = name == "own" or event(slot) == s
                            code |= (names[s].index(name) if near else len(names[s]) + where) << shift
                        local = 0 if kind == 0 else 1 + [i for i, x in enumerate(SENDS) if x[0] == s].index(kind - 1)
                        line[bases[s] + 1 + t] = code | local << 12 | place << 16
                    moved = sorted(keeps.get((r, j, y, s), ()))
                    line[kept_bases[s]] = len(moved)
                    for t, (name, where) in enumerate(moved):
                        line[kept_bases[s] + 1 + t] = names[s].index(name) | where << 6
                for i in range(half):
                    for kc in range(n):
                        index, place = arrives[r, j, y, y * half + i, kc]
                        line[final + i * n + kc] = index | place << 4

    def permute(x, pairs):
        return lax.ppermute(x, ("row", "col"), [(a[0] * n + a[1], b[0] * n + b[1]) for a, b in pairs])

    def tie(x, *others):
        return lax.optimization_barrier((x, *others))[0] if others else x

    def local(velocity, panel_weight, panel_group, tile_map, group_gain):
        place = lax.axis_index("row"), lax.axis_index("col"), lax.axis_index("panel")
        line = lax.dynamic_slice(jnp.asarray(table), (*place, 0), (1, 1, 1, size)).reshape(size)
        have = {"own": jnp.transpose(velocity, (1, 0, 2))}
        weight, group = panel_weight[None, :], panel_group[None, :]
        own, kept, recvs, sents = None, None, [], {}
        last = max(s for s, _, _ in moves.values())
        for slot in range(0, last + 2):
            held = [have[k] for k, m in moves.items() if m[0] == slot - 1 and k != "own"]
            done = sents.get(slot - 2, [])
            for name, (s, source, pairs) in moves.items():
                if s == slot and source is not None:
                    x = have[source]
                    have[name] = permute(tie(x, *done, *(held if name[0] == "q" else [])), pairs)
            for name, (s, source, pairs) in spreads.items():
                if s == slot:
                    have[name] = permute(tie(have[source], *done), pairs)
            if slot not in slots:
                continue
            caps = [c for s, c in SENDS if s == slot]
            first = own is None
            used = [have[k] for k in names[slot]]
            anywhere = pl.BlockSpec(memory_space=pltpu.HBM)
            flops = 4 * 2 * h * h * 6 * p * max(1, most[slot] // 2)
            made = pl.pallas_call(
                functools.partial(multiply_blocks, first, bases[slot], kept_bases[slot], len(used), caps, h, p, gap),
                out_shape=[
                    jax.ShapeDtypeStruct((half * n, block, LANES), jnp.float32),
                    jax.ShapeDtypeStruct((2 * n, 6, h, p), jnp.bfloat16),
                ]
                + [jax.ShapeDtypeStruct((c, block, LANES), jnp.bfloat16) for c in caps],
                in_specs=[pl.BlockSpec(memory_space=pltpu.SMEM)] * 3
                + [pl.BlockSpec(memory_space=pltpu.VMEM)] * 2
                + [anywhere] * (len(used) + (0 if first else 2)),
                out_specs=[anywhere] * (2 + len(caps)),
                input_output_aliases={} if first else {5 + len(used): 0, 6 + len(used): 1},
                scratch_shapes=[
                    pltpu.VMEM((2 * h, 3 * p), jnp.bfloat16),
                    pltpu.VMEM((2, gap + h, 3 * p), jnp.bfloat16),
                    pltpu.VMEM((block, LANES), jnp.float32),
                    pltpu.VMEM((block, LANES), jnp.bfloat16),
                    pltpu.SemaphoreType.DMA,
                    pltpu.SemaphoreType.DMA((2,)),
                    pltpu.SemaphoreType.DMA,
                    pltpu.SemaphoreType.DMA,
                ],
                compiler_params=pltpu.CompilerParams(vmem_limit_bytes=60 << 20),
                cost_estimate=pl.CostEstimate(flops=flops, bytes_accessed=8 << 20, transcendentals=0),
                name=f"blocks_{slot}",
            )(line, tile_map, group_gain, weight, group, *used, *([] if first else [own, kept]))
            own, kept = made[:2]
            sents[slot] = made[2:3]
            for sent in made[2:]:
                pairs = []
                for r, j, y in send_pairs[len(recvs)]:
                    pairs.append(((r * n + j) * 2 + y, (r * n + j) * 2 + 1 - y))
                recvs.append(lax.ppermute(sent, ("row", "col", "panel"), pairs))
        wide = n * h // LANES
        return pl.pallas_call(
            functools.partial(add_up, final, n, h),
            out_shape=jax.ShapeDtypeStruct((half * h, 2, n * h), jnp.float32),
            in_specs=[pl.BlockSpec(memory_space=pltpu.SMEM)]
            + [pl.BlockSpec(memory_space=pltpu.HBM)] * (1 + len(recvs)),
            out_specs=pl.BlockSpec(memory_space=pltpu.HBM),
            scratch_shapes=[
                pltpu.VMEM((2, block, LANES), jnp.float32),
                pltpu.VMEM((2, block, LANES), jnp.bfloat16),
                pltpu.VMEM((h, n * h), jnp.float32),
                pltpu.VMEM((h, n * h), jnp.float32),
                pltpu.VMEM((2, h * 2 * wide, LANES), jnp.float32),
                pltpu.SemaphoreType.DMA((2,)),
                pltpu.SemaphoreType.DMA((2,)),
                pltpu.SemaphoreType.DMA((2,)),
            ],
            compiler_params=pltpu.CompilerParams(vmem_limit_bytes=60 << 20),
            name="add_up",
        )(line, own, *recvs)

    return local


def contract(left_side, right_side):
    return lax.dot_general(
        left_side, right_side, (((1,), (1,)), ((), ())), preferred_element_type=jnp.float32
    )


def plain(velocity, panel_weight, panel_group, tile_map, group_gain):
    row_index, col_index = lax.axis_index("row"), lax.axis_index("col")
    rows_block = lax.all_gather(velocity, "col", axis=0, tiled=True)
    kept = jnp.where(row_index == col_index, rows_block, 0).astype(rows_block.dtype)
    cols_block = lax.psum(kept, "row")
    gains = lax.dynamic_index_in_dim(group_gain, tile_map[row_index, col_index], 1, keepdims=False)
    scale = panel_weight * gains[panel_group]
    weighted = (rows_block.astype(jnp.float32) * scale[None, None, :]).astype(jnp.bfloat16)
    width, depth = weighted.shape[0], 3 * weighted.shape[2]
    left = weighted.reshape(width, 2 * depth)
    right = cols_block.reshape(width, 2 * depth)
    sign = jnp.where(row_index <= col_index, jnp.float32(1.0), jnp.float32(-1.0))
    real = contract(left[:, :depth], right[:, :depth]) + sign * contract(left[:, depth:], right[:, depth:])
    imag = contract(left[:, depth:], right[:, :depth]) - sign * contract(left[:, :depth], right[:, depth:])
    return lax.psum_scatter(jnp.stack((real, imag), axis=1), "panel", scatter_dimension=0, tiled=True)


def solution(mesh):
    n, panels = mesh.shape["col"], mesh.shape["panel"]

    def whole(velocity, panel_weight, panel_group, tile_map, group_gain):
        h = velocity.shape[0] // (n * n)
        p = velocity.shape[2] // panels
        fits = (
            mesh.shape["row"] == n
            and n == 4
            and panels == 2
            and h % 32 == 0
            and (h % LANES) * 4 == LANES
            and (n * h) % LANES == 0
            and p % LANES == 0
        )
        return jax.shard_map(
            tiled(mesh, h, p) if fits else plain,
            mesh=mesh,
            in_specs=(P(("row", "col"), None, "panel"), P("panel"), P("panel"), P(), P()),
            out_specs=P(("row", "panel"), None, "col"),
            check_vma=False,
        )(velocity, panel_weight, panel_group, tile_map, group_gain)

    return whole
```

```python
import functools

import jax
import jax.numpy as jnp
import numpy as np
from jax import lax
from jax.experimental import pallas as pl
from jax.experimental.pallas import tpu as pltpu
from jax.sharding import PartitionSpec as P

LANES = 128
ARRIVALS = (
    (("own", "a", "b", "x0", "c0", "ca", "cb", "d0"), 5),
    (("xb",), 5),
    (("t", "xa", "da", "db"), 5),
    (("ct",), 4),
    (("e", "xt"), 3),
    (("dt",), 3),
    ((), 16),
)
SENDS = ((0, 3), (1, 3), (2, 2), (3, 2), (4, 2), (5, 3))


def route(n):
    devices = [(r, j) for r in range(n) for j in range(n)]
    holds = {"own": {d: d[1] for d in devices}}
    pairs, source = {}, {}

    def add(name, operand, moves):
        pairs[name], source[name] = moves, operand
        holds[name] = {t: holds[operand][f] for f, t in moves}

    ends = [(r, j) for r, j in devices if j in (0, n - 1)]
    inner = [d for d in devices if d not in ends]
    early = [(r, j) for r, j in ends if (r + j) % 2 == 0]
    add("a", "own", [((r, j ^ 1), (r, j)) for r, j in devices])
    add("b", "own", [((r, j ^ 3), (r, j)) for r, j in inner + early])
    holds["z"] = {(r, j): j ^ 3 if (r, j) in inner else j for r, j in devices}
    add("t", "z", [((r, j ^ (1 if (r, j) in ends else 2)), (r, j)) for r, j in devices])
    del holds["z"]
    add("e", "t", [((r, j ^ 1), (r, j)) for r, j in ends if (r, j) not in early])
    rows = {d: {} for d in devices}
    cols = {d: {} for d in devices}
    for name, held in holds.items():
        for device, plane in held.items():
            assert plane not in rows[device]
            rows[device][plane] = name
    for e, name in (("0", "own"), ("a", "a"), ("b", "b"), ("t", "t")):
        for v, kind in ((0, ""), (2, "x"), (1, "c"), (3, "d")):
            parent = 2 if v == 3 else 0
            if v:
                pairs[kind + e] = [((c ^ parent, c), (c ^ v, c)) for c in range(n)]
                source[kind + e] = "x" + e if parent else name
            for c in range(n):
                cols[c ^ v, c][holds[name][c, c]] = kind + e if v else name
    assert all(len(x) == n for d in devices for x in (rows[d], cols[d]))
    return pairs, source, rows, cols


def share_out(n, rows, cols):
    half = n // 2
    event = {name: e for e, (names, _) in enumerate(ARRIVALS) for name in names}
    window = [min((i for i, x in enumerate(SENDS) if x[0] >= e), default=None) for e in range(len(ARRIVALS))]
    tasks, senders, arrives = {}, [[] for _ in SENDS], {}

    def attempt(blocks, chosen):
        wait, plan = list(blocks), []
        room = [x[1] if i in chosen else 0 for i, x in enumerate(SENDS)]
        for e, (_, most) in enumerate(ARRIVALS):
            i = window[e]
            now = [b for b in wait if b[0] <= e]
            leave = [] if i is None else [b for b in now if not b[1]][:min(most, room[i])]
            if leave:
                room[i] -= len(leave)
            stay = [b for b in now if b[1]][:most - len(leave)]
            for b in leave + stay:
                wait.remove(b)
                plan.append((e, i if b in leave else None, b[2], b[3]))
        return None if wait else plan

    for r in range(n):
        for j in range(n):
            for y in range(2):
                blocks = sorted(
                    (max(event[rows[r, j][kr]], event[cols[r, j][kc]]), kr // half == y, kr, kc)
                    for kr in range(n)
                    for kc in range(n)
                )
                best = None
                for mask in range(1 << len(SENDS)):
                    chosen = [i for i in range(len(SENDS)) if mask >> i & 1]
                    plan = attempt(blocks, chosen)
                    if plan is None:
                        continue
                    cost = sum(SENDS[i][1] * (1 + i) ** 2 for i in chosen), sum(e for e, i, _, _ in plan if i is not None)
                    if best is None or cost < best[0]:
                        best = cost, plan
                used = {}
                for e, i, kr, kc in best[1]:
                    if i is None:
                        place = (kr - y * half) * n + kc
                    else:
                        place = used[i] = used.get(i, -1) + 1
                        arrives[r, j, 1 - y, kr, kc] = i, place
                    tasks.setdefault((r, j, y, e), []).append((kr, kc, int(i is not None), place))
                for i in used:
                    senders[i].append((r, j, y))
    return tasks, senders, arrives


def rate(w_ref, group_ref, gain_ref, region):
    groups = group_ref[...]
    gain = jnp.zeros(groups.shape, jnp.float32)
    for g in range(gain_ref.shape[0]):
        gain = gain + jnp.where(groups == g, gain_ref[g, region], jnp.float32(0.0))
    return w_ref[...] * gain


def fetch(index, sources, target, sem, h, p, gap):
    for i, source in enumerate(sources):

        @pl.when(index == i)
        def _():
            for c in range(6):
                pltpu.make_async_copy(
                    source.at[c], target.at[pl.ds((c // 3) * gap, h), pl.ds((c % 3) * p, p)], sem
                ).start()


def landed(sources, target, sem, h, p, gap):
    for c in range(6):
        pltpu.make_async_copy(
            sources[0].at[c], target.at[pl.ds((c // 3) * gap, h), pl.ds((c % 3) * p, p)], sem
        ).wait()


def pack(stage, real, imag, h):
    tail, quarter = h % LANES, h // 2
    full = h // LANES
    for part, value in ((0, real), (1, imag)):
        for k in range(full):
            stage[pl.ds((part * full + k) * h, h), :] = value[:, k * LANES:(k + 1) * LANES].astype(stage.dtype)
        for fold in range(2):
            lane = (2 * fold + part) * tail
            stage[pl.ds(2 * full * h, quarter), lane:lane + tail] = value[
                fold * quarter:(fold + 1) * quarter, full * LANES:
            ].astype(stage.dtype)


def pick(second, first_ref, second_ref, out, held, sem):
    for k, source in enumerate((first_ref, second_ref)):

        @pl.when(second[0] == k)
        def _():
            pltpu.make_async_copy(source, held, sem).start()

    pltpu.make_async_copy(first_ref, held, sem).wait()
    copy = pltpu.make_async_copy(held, out, sem)
    copy.start()
    copy.wait()


def multiply_blocks(passed, results, base, sources, h, p, gap, table, tile_map, gain_ref, w_ref, group_ref, *refs):
    srcs = refs[:sources]
    refs = refs[sources + passed:]
    own, out = refs[0], refs[results - 1]
    raw, left, right, stage_own, stage_out, l_sem, r_sem, own_sem, out_sem = refs[results:]
    count = table[base]
    sign = table[2].astype(jnp.float32)
    scale = rate(w_ref, group_ref, gain_ref, tile_map[table[0], table[1]])

    def entry(t):
        code = table[base + 1 + t]
        return code & 63, (code >> 6) & 63, (code >> 12) & 15, code >> 16

    def stored(stage, target, sem, slot, place):
        return pltpu.make_async_copy(stage.at[slot], target.at[place], sem.at[slot])

    def store(stage, target, sem, done, place, real, imag):
        slot = lax.rem(done, 2)

        @pl.when(done > 1)
        def _():
            stored(stage, target, sem, slot, 0).wait()

        pack(stage.at[slot], real, imag, h)
        stored(stage, target, sem, slot, place).start()

    def settle(stage, target, sem, done):
        for back in (1, 2):

            @pl.when(done >= back)
            def _():
                stored(stage, target, sem, lax.rem(done - back, 2), 0).wait()

    def ask_row(t):
        fetch(entry(t)[0], srcs, raw.at[lax.rem(t, 2)], l_sem.at[lax.rem(t, 2)], h, p, h)

    def ask_column(t):
        fetch(entry(t)[1], srcs, right.at[lax.rem(t, 2)], r_sem.at[lax.rem(t, 2)], h, p, gap)

    def weigh(slot):
        for c in range(3):
            part = raw[slot, :, c * p:(c + 1) * p].astype(jnp.float32)
            left[slot, :, c * p:(c + 1) * p] = (part * scale).astype(jnp.bfloat16)

    @pl.when(count > 0)
    def _():
        ask_row(0)
        ask_column(0)

        @pl.when(count > 1)
        def _():
            ask_row(1)

        landed(srcs, raw.at[0], l_sem.at[0], h, p, h)
        weigh(0)

    def task(t, carry):
        owns, outs = carry
        _, _, kind, place = entry(t)
        slot = lax.rem(t, 2)
        other = 1 - slot

        @pl.when(t + 1 < count)
        def _():
            landed(srcs, raw.at[other], l_sem.at[other], h, p, h)
            ask_column(t + 1)

        @pl.when(t + 2 < count)
        def _():
            ask_row(t + 2)

        landed(srcs, right.at[slot], r_sem.at[slot], h, p, gap)
        weigh(other)
        product = lax.dot_general(
            left[slot], right[slot], (((1,), (1,)), ((), ())), preferred_element_type=jnp.float32
        )
        real = product[:h, :h] + sign * product[h:, gap:gap + h]
        imag = product[h:, :h] - sign * product[:h, gap:gap + h]

        @pl.when(kind == 0)
        def _():
            store(stage_own, own, own_sem, owns, place, real, imag)

        if results > 1:

            @pl.when(kind == 1)
            def _():
                store(stage_out, out, out_sem, outs, place, real, imag)

        return owns + (kind == 0).astype(jnp.int32), outs + (kind == 1).astype(jnp.int32)

    zero = jnp.int32(0)
    owns, outs = lax.fori_loop(0, count, task, (zero, zero))
    settle(stage_own, own, own_sem, owns)
    if results > 1:
        settle(stage_out, out, out_sem, outs)


def add_up(base, n, h, table, own, *refs):
    recvs = refs[:len(SENDS)]
    out, mine, theirs, real, imag, image, m_sem, t_sem, o_sem = refs[len(SENDS):]
    blocks = (n // 2) * n
    full, tail, quarter = h // LANES, h % LANES, h // 2
    wide = n * h // LANES

    def load(b, slot):
        pltpu.make_async_copy(own.at[b], mine.at[slot], m_sem.at[slot]).start()
        code = table[base + b]
        for k, recv in enumerate(recvs):

            @pl.when((code & 15) == k)
            def _():
                pltpu.make_async_copy(recv.at[code >> 4], theirs.at[slot], t_sem.at[slot]).start()

    def written(chunk, k):
        return pltpu.make_async_copy(
            image.at[chunk % 2, pl.ds(2 * k * h, 2 * h)].reshape(h, 2, LANES),
            out.at[pl.ds(chunk * h, h), :, pl.ds(k * LANES, LANES)],
            o_sem.at[chunk % 2],
        )

    load(0, 0)
    for b in range(blocks):
        slot, chunk, kc = b % 2, b // n, b % n
        if b + 1 < blocks:
            load(b + 1, 1 - slot)
        pltpu.make_async_copy(own.at[0], mine.at[slot], m_sem.at[slot]).wait()
        pltpu.make_async_copy(recvs[0].at[0], theirs.at[slot], t_sem.at[slot]).wait()
        for part, line in ((0, real), (1, imag)):
            for k in range(full):
                at = pl.ds((part * full + k) * h, h)
                line[:, kc * h + k * LANES:kc * h + (k + 1) * LANES] = mine[slot, at, :] + theirs[
                    slot, at, :
                ].astype(jnp.float32)
            at = pl.ds(2 * full * h, quarter)
            rest = mine[slot, at, :] + theirs[slot, at, :].astype(jnp.float32)
            for fold in range(2):
                lane = (2 * fold + part) * tail
                line[
                    fold * quarter:(fold + 1) * quarter, kc * h + full * LANES:(kc + 1) * h
                ] = rest[:, lane:lane + tail]
        if kc == n - 1:
            buf = chunk % 2
            for part, line in ((0, real), (1, imag)):
                for k in range(wide):
                    image[buf, pl.ds(2 * k * h + part, h, stride=2), :] = line[:, k * LANES:(k + 1) * LANES]
            for k in range(wide):
                written(chunk, k).start()
    for chunk in range(n // 2):
        for k in range(wide):
            written(chunk, k).wait()


def tiled(mesh, h, p):
    n = mesh.shape["col"]
    half = n // 2
    pairs, source, rows, cols = route(n)
    tasks, senders, arrives = share_out(n, rows, cols)
    gap = -(-h // LANES) * LANES
    block = 2 * h * h // LANES
    events = range(len(ARRIVALS))

    names = {e: set() for e in events}
    for (r, j, _, e), items in tasks.items():
        for kr, kc, _, _ in items:
            names[e] |= {rows[r, j][kr], cols[r, j][kc]}
    names = {e: sorted(v) for e, v in names.items()}
    bases, size = {}, 3
    for e in events:
        bases[e] = size
        size += 1 + max(len(v) for k, v in tasks.items() if k[3] == e)
    final = size
    size += half * n
    table = np.zeros((n, n, 2, size), np.int32)
    for r in range(n):
        for j in range(n):
            for y in range(2):
                line = table[r, j, y]
                line[:3] = r, j, 1 if r <= j else -1
                for e in events:
                    items = sorted(tasks.get((r, j, y, e), []), key=lambda i: (names[e].index(rows[r, j][i[0]]), -i[2], i[3]))
                    line[bases[e]] = len(items)
                    for t, (kr, kc, kind, place) in enumerate(items):
                        parts = names[e].index(rows[r, j][kr]) | names[e].index(cols[r, j][kc]) << 6
                        line[bases[e] + 1 + t] = parts | kind << 12 | place << 16
                for i in range(half):
                    for kc in range(n):
                        index, place = arrives[r, j, y, y * half + i, kc]
                        line[final + i * n + kc] = index | place << 4

    def local(velocity, panel_weight, panel_group, tile_map, group_gain):
        here = lax.axis_index("row"), lax.axis_index("col"), lax.axis_index("panel")
        line = lax.dynamic_slice(jnp.asarray(table), (*here, 0), (1, 1, 1, size)).reshape(size)
        weight, group = panel_weight[None, :], panel_group[None, :]
        have = {"own": jnp.transpose(velocity, (1, 0, 2))}
        anywhere = pl.BlockSpec(memory_space=pl.ANY)

        def move(*given):
            for name in given:
                with jax.named_scope("move_" + name):
                    ids = [(a[0] * n + a[1], b[0] * n + b[1]) for a, b in pairs[name]]
                    have[name] = lax.ppermute(have[source[name]], ("row", "col"), ids)

        def choose(name, first, second):
            inner = jnp.logical_and(here[1] > 0, here[1] < n - 1).astype(jnp.int32)[None]
            have[name] = pl.pallas_call(
                pick,
                out_shape=jax.ShapeDtypeStruct((6, h, p), jnp.bfloat16),
                in_specs=[pl.BlockSpec(memory_space=pltpu.SMEM)] + [anywhere] * 2,
                out_specs=anywhere,
                scratch_shapes=[pltpu.VMEM((6, h, p), jnp.bfloat16), pltpu.SemaphoreType.DMA],
                compiler_params=pltpu.CompilerParams(vmem_limit_bytes=60 << 20),
                cost_estimate=pl.CostEstimate(flops=1 << 10, bytes_accessed=1 << 10, transcendentals=0),
                name="pick",
            )(inner, have[first], have[second])

        def fence(*wanted):
            keys = list(dict.fromkeys(wanted))
            have.update(zip(keys, lax.optimization_barrier(tuple(have[k] for k in keys))))

        def blocks(e):
            boxes = [i for i, x in enumerate(SENDS) if x[0] >= e][:1]
            results = ["sums"] + [f"sent{i}" for i in boxes]
            used = [have[k] for k in names[e]]
            carried = [(k, i) for i, k in enumerate(results) if k in have]
            made = pl.pallas_call(
                functools.partial(multiply_blocks, len(carried), len(results), bases[e], len(used), h, p, gap),
                out_shape=[jax.ShapeDtypeStruct((half * n, block, LANES), jnp.float32)]
                + [jax.ShapeDtypeStruct((SENDS[i][1], block, LANES), jnp.bfloat16) for i in boxes],
                in_specs=[pl.BlockSpec(memory_space=pltpu.SMEM)] * 3
                + [pl.BlockSpec(memory_space=pltpu.VMEM)] * 2
                + [anywhere] * (len(used) + len(carried)),
                out_specs=[anywhere] * len(results),
                input_output_aliases={5 + len(used) + at: i for at, (_, i) in enumerate(carried)},
                scratch_shapes=[
                    pltpu.VMEM((2, 2 * h, 3 * p), jnp.bfloat16),
                    pltpu.VMEM((2, 2 * h, 3 * p), jnp.bfloat16),
                    pltpu.VMEM((2, gap + h, 3 * p), jnp.bfloat16),
                    pltpu.VMEM((2, block, LANES), jnp.float32),
                    pltpu.VMEM((2, block, LANES), jnp.bfloat16),
                    pltpu.SemaphoreType.DMA((2,)),
                    pltpu.SemaphoreType.DMA((2,)),
                    pltpu.SemaphoreType.DMA((2,)),
                    pltpu.SemaphoreType.DMA((2,)),
                ],
                compiler_params=pltpu.CompilerParams(vmem_limit_bytes=60 << 20),
                cost_estimate=pl.CostEstimate(flops=1 << 20, bytes_accessed=1 << 16, transcendentals=0),
                name=f"blocks_{e}",
            )(line, tile_map, group_gain, weight, group, *used, *(have[k] for k, _ in carried))
            have.update(zip(results, made))

        def exchange(i):
            ids = [((r * n + j) * 2 + y, (r * n + j) * 2 + 1 - y) for r, j, y in senders[i]]
            with jax.named_scope(f"move_sums{i}"):
                have[f"got{i}"] = lax.ppermute(have[f"sent{i}"], ("row", "col", "panel"), ids)

        move("c0", "x0", "b", "a")
        fence("own", "b", "a", "x0", "c0")
        choose("z", "own", "b")
        move("t", "xa", "xb", "ca", "cb", "d0")
        fence("d0", "ca", "cb")
        blocks(0)
        fence("sums", "sent0", "xb")
        exchange(0)
        blocks(1)
        fence("sums", "sent1", "got0", "xa", "t")
        move("e", "xt", "ct", "da", "db")
        exchange(1)
        fence("da", "db")
        blocks(2)
        fence("sums", "sent2", "ct")
        exchange(2)
        blocks(3)
        fence("sums", "sent3", "got1", "got2", "xt", "e")
        exchange(3)
        move("dt")
        blocks(4)
        fence("dt", "sums", "sent4")
        exchange(4)
        blocks(5)
        fence("sums", "sent5", "got3", "got4")
        exchange(5)
        blocks(6)
        got = [have[f"got{i}"] for i in range(len(SENDS))]
        return pl.pallas_call(
            functools.partial(add_up, final, n, h),
            out_shape=jax.ShapeDtypeStruct((half * h, 2, n * h), jnp.float32),
            in_specs=[pl.BlockSpec(memory_space=pltpu.SMEM)] + [anywhere] * (1 + len(got)),
            out_specs=anywhere,
            scratch_shapes=[
                pltpu.VMEM((2, block, LANES), jnp.float32),
                pltpu.VMEM((2, block, LANES), jnp.bfloat16),
                pltpu.VMEM((h, n * h), jnp.float32),
                pltpu.VMEM((h, n * h), jnp.float32),
                pltpu.VMEM((2, 2 * h * n * h // LANES, LANES), jnp.float32),
                pltpu.SemaphoreType.DMA((2,)),
                pltpu.SemaphoreType.DMA((2,)),
                pltpu.SemaphoreType.DMA((2,)),
            ],
            compiler_params=pltpu.CompilerParams(vmem_limit_bytes=60 << 20),
            name="add_up",
        )(line, have["sums"], *got)

    return local


def contract(left_side, right_side):
    return lax.dot_general(
        left_side, right_side, (((1,), (1,)), ((), ())), preferred_element_type=jnp.float32
    )


def plain(velocity, panel_weight, panel_group, tile_map, group_gain):
    row_index, col_index = lax.axis_index("row"), lax.axis_index("col")
    rows_block = lax.all_gather(velocity, "col", axis=0, tiled=True)
    kept = jnp.where(row_index == col_index, rows_block, 0).astype(rows_block.dtype)
    cols_block = lax.psum(kept, "row")
    gains = lax.dynamic_index_in_dim(group_gain, tile_map[row_index, col_index], 1, keepdims=False)
    scale = panel_weight * gains[panel_group]
    weighted = (rows_block.astype(jnp.float32) * scale[None, None, :]).astype(jnp.bfloat16)
    width, depth = weighted.shape[0], 3 * weighted.shape[2]
    left = weighted.reshape(width, 2 * depth)
    right = cols_block.reshape(width, 2 * depth)
    sign = jnp.where(row_index <= col_index, jnp.float32(1.0), jnp.float32(-1.0))
    real = contract(left[:, :depth], right[:, :depth]) + sign * contract(left[:, depth:], right[:, depth:])
    imag = contract(left[:, depth:], right[:, :depth]) - sign * contract(left[:, :depth], right[:, depth:])
    return lax.psum_scatter(jnp.stack((real, imag), axis=1), "panel", scatter_dimension=0, tiled=True)


def solution(mesh):
    n, panels = mesh.shape["col"], mesh.shape["panel"]

    def whole(velocity, panel_weight, panel_group, tile_map, group_gain):
        h = velocity.shape[0] // (n * n)
        p = velocity.shape[2] // panels
        fits = (
            mesh.shape["row"] == n
            and n == 4
            and panels == 2
            and h % 32 == 0
            and (h % LANES) * 4 == LANES
            and (n * h) % LANES == 0
            and p % LANES == 0
        )
        return jax.shard_map(
            tiled(mesh, h, p) if fits else plain,
            mesh=mesh,
            in_specs=(P(("row", "col"), None, "panel"), P("panel"), P("panel"), P(), P()),
            out_specs=P(("row", "panel"), None, "col"),
            check_vma=False,
        )(velocity, panel_weight, panel_group, tile_map, group_gain)

    return whole
```

```python
import functools

import jax
import jax.numpy as jnp
import numpy as np
from jax import lax
from jax.experimental import pallas as pl
from jax.experimental.pallas import tpu as pltpu
from jax.sharding import PartitionSpec as P

LANES = 128
KNOWN = 32
ARRIVALS = (
    (("own", "a", "b", "x0", "c0", "ca", "cb", "d0", "xa"), 5),
    (("xb",), 6),
    (("t", "da", "db"), 3),
    (("ct",), 4),
    (("e", "xt"), 2),
    (("dt",), 3),
    ((), 16),
)
SENDS = ((0, 3), (1, 2), (2, 2), (3, 2), (4, 2), (5, 3))


def route(n):
    devices = [(r, j) for r in range(n) for j in range(n)]
    holds = {"own": {d: d[1] for d in devices}}
    pairs, source = {}, {}

    def add(name, operand, moves):
        pairs[name], source[name] = moves, operand
        holds[name] = {t: holds[operand][f] for f, t in moves}

    ends = [(r, j) for r, j in devices if j in (0, n - 1)]
    inner = [d for d in devices if d not in ends]
    early = [(r, j) for r, j in ends if (r + j) % 2 == 0]
    add("a", "own", [((r, j ^ 1), (r, j)) for r, j in devices])
    add("b", "own", [((r, j ^ 3), (r, j)) for r, j in inner + early])
    holds["z"] = {(r, j): j ^ 3 if (r, j) in inner else j for r, j in devices}
    add("t", "z", [((r, j ^ (1 if (r, j) in ends else 2)), (r, j)) for r, j in devices])
    del holds["z"]
    add("e", "t", [((r, j ^ 1), (r, j)) for r, j in ends if (r, j) not in early])
    rows = {d: {} for d in devices}
    cols = {d: {} for d in devices}
    for name, held in holds.items():
        for device, plane in held.items():
            assert plane not in rows[device]
            rows[device][plane] = name
    for e, name in (("0", "own"), ("a", "a"), ("b", "b"), ("t", "t")):
        for v, kind in ((0, ""), (2, "x"), (1, "c"), (3, "d")):
            parent = 2 if v == 3 else 0
            if v:
                pairs[kind + e] = [((c ^ parent, c), (c ^ v, c)) for c in range(n)]
                source[kind + e] = "x" + e if parent else name
            for c in range(n):
                cols[c ^ v, c][holds[name][c, c]] = kind + e if v else name
    assert all(len(x) == n for d in devices for x in (rows[d], cols[d]))
    return pairs, source, rows, cols


def share_out(n, rows, cols):
    half = n // 2
    event = {name: e for e, (names, _) in enumerate(ARRIVALS) for name in names}
    window = [min((i for i, x in enumerate(SENDS) if x[0] >= e), default=None) for e in range(len(ARRIVALS))]
    tasks, senders, arrives = {}, [[] for _ in SENDS], {}

    def attempt(blocks, chosen):
        wait, plan = list(blocks), []
        room = [x[1] if i in chosen else 0 for i, x in enumerate(SENDS)]
        for e, (_, most) in enumerate(ARRIVALS):
            i = window[e]
            now = [b for b in wait if b[0] <= e]
            leave = [] if i is None else [b for b in now if not b[1]][:min(most, room[i])]
            if leave:
                room[i] -= len(leave)
            stay = [b for b in now if b[1]][:most - len(leave)]
            for b in leave + stay:
                wait.remove(b)
                plan.append((e, i if b in leave else None, b[2], b[3]))
        return None if wait else plan

    for r in range(n):
        for j in range(n):
            for y in range(2):
                blocks = sorted(
                    (max(event[rows[r, j][kr]], event[cols[r, j][kc]]), kr // half == y, kr, kc)
                    for kr in range(n)
                    for kc in range(n)
                )
                best = None
                for mask in range(1 << len(SENDS)):
                    chosen = [i for i in range(len(SENDS)) if mask >> i & 1]
                    plan = attempt(blocks, chosen)
                    if plan is None:
                        continue
                    cost = sum(SENDS[i][1] * i**2 for i in chosen), sum(e * e for e, _, _, _ in plan)
                    if best is None or cost < best[0]:
                        best = cost, plan
                used = {}
                for e, i, kr, kc in best[1]:
                    if i is None:
                        place = (kr - y * half) * n + kc
                    else:
                        place = used[i] = used.get(i, -1) + 1
                        arrives[r, j, 1 - y, kr, kc] = i, place
                    tasks.setdefault((r, j, y, e), []).append((kr, kc, int(i is not None), place))
                for i in used:
                    senders[i].append((r, j, y))
    return tasks, senders, arrives


def rate(w_ref, group_ref, gain_ref, region):
    groups = group_ref[...]
    gain = jnp.zeros(groups.shape, jnp.float32)
    for g in range(gain_ref.shape[0]):
        gain = gain + jnp.where(groups == g, gain_ref[g, region], jnp.float32(0.0))
    return w_ref[...] * gain


def fetch(index, sources, target, sem, h, p, gap):
    for i, source in enumerate(sources):

        @pl.when(index == i)
        def _():
            for c in range(6):
                pltpu.make_async_copy(
                    source.at[c], target.at[pl.ds((c // 3) * gap, h), pl.ds((c % 3) * p, p)], sem
                ).start()


def landed(sources, target, sem, h, p, gap):
    for c in range(6):
        pltpu.make_async_copy(
            sources[0].at[c], target.at[pl.ds((c // 3) * gap, h), pl.ds((c % 3) * p, p)], sem
        ).wait()


def pack(stage, real, imag, h):
    tail, quarter = h % LANES, h // 2
    full = h // LANES
    for part, value in ((0, real), (1, imag)):
        for k in range(full):
            stage[pl.ds((part * full + k) * h, h), :] = value[:, k * LANES:(k + 1) * LANES].astype(stage.dtype)
        for fold in range(2):
            lane = (2 * fold + part) * tail
            stage[pl.ds(2 * full * h, quarter), lane:lane + tail] = value[
                fold * quarter:(fold + 1) * quarter, full * LANES:
            ].astype(stage.dtype)


def pick(second, first_ref, second_ref, out, held, sem):
    for k, source in enumerate((first_ref, second_ref)):

        @pl.when(second[0] == k)
        def _():
            pltpu.make_async_copy(source, held, sem).start()

    pltpu.make_async_copy(first_ref, held, sem).wait()
    copy = pltpu.make_async_copy(held, out, sem)
    copy.start()
    copy.wait()


def multiply_blocks(passed, results, base, sources, h, p, gap, table, tile_map, gain_ref, w_ref, group_ref, *refs):
    srcs = refs[:sources]
    refs = refs[sources + passed:]
    own, weighed, out = refs[0], refs[1], refs[results - 1]
    raw, left, right, stage_own, stage_out, raw_sem, l_sem, w_sem, r_sem, own_sem, out_sem = refs[results:]
    count = table[base]
    sign = table[2].astype(jnp.float32)
    scale = rate(w_ref, group_ref, gain_ref, tile_map[table[0], table[1]])

    def entry(t):
        code = table[base + 1 + t]
        return code & 63, (code >> 6) & 63, (code >> 12) & 15, (code >> 16) & 255, code >> 24

    def stored(stage, target, sem, slot, place):
        return pltpu.make_async_copy(stage.at[slot], target.at[place], sem.at[slot])

    def store(stage, target, sem, done, place, real, imag):
        slot = lax.rem(done, 2)

        @pl.when(done > 1)
        def _():
            stored(stage, target, sem, slot, 0).wait()

        pack(stage.at[slot], real, imag, h)
        stored(stage, target, sem, slot, place).start()

    def settle(stage, target, sem, done):
        for back in (1, 2):

            @pl.when(done >= back)
            def _():
                stored(stage, target, sem, lax.rem(done - back, 2), 0).wait()

    def known(slot, plane):
        return pltpu.make_async_copy(weighed.at[plane], left.at[slot], l_sem.at[slot])

    def kept(slot, plane):
        return pltpu.make_async_copy(left.at[slot], weighed.at[plane], w_sem)

    def ask_row(t, slot):
        row, plane = entry(t)[0], entry(t)[4]
        fetch(row, srcs, raw, raw_sem, h, p, h)

        @pl.when(row >= KNOWN)
        def _():
            known(slot, plane).start()

    def ask_column(t):
        fetch(entry(t)[1], srcs, right.at[lax.rem(t, 2)], r_sem.at[lax.rem(t, 2)], h, p, gap)

    @pl.when(count > 0)
    def _():
        ask_row(0, 0)
        ask_column(0)

    def task(t, carry):
        before, side, owns, outs = carry
        row, _, kind, place, plane = entry(t)
        slot = lax.rem(t, 2)
        changed = plane != before
        side = jnp.where(changed, 1 - side, side)
        fresh = jnp.logical_and(changed, row < KNOWN)

        @pl.when(jnp.logical_and(changed, row >= KNOWN))
        def _():
            known(side, plane).wait()

        @pl.when(fresh)
        def _():
            landed(srcs, raw, raw_sem, h, p, h)
            for c in range(3):
                part = raw[:, c * p:(c + 1) * p].astype(jnp.float32)
                left[side, :, c * p:(c + 1) * p] = (part * scale).astype(jnp.bfloat16)
            kept(side, plane).start()

        @pl.when(t + 1 < count)
        def _():
            ask_column(t + 1)

            @pl.when(entry(t + 1)[4] != plane)
            def _():
                ask_row(t + 1, 1 - side)

        landed(srcs, right.at[slot], r_sem.at[slot], h, p, gap)
        product = lax.dot_general(
            left[side], right[slot], (((1,), (1,)), ((), ())), preferred_element_type=jnp.float32
        )
        real = product[:h, :h] + sign * product[h:, gap:gap + h]
        imag = product[h:, :h] - sign * product[:h, gap:gap + h]

        @pl.when(fresh)
        def _():
            kept(side, plane).wait()

        @pl.when(kind == 0)
        def _():
            store(stage_own, own, own_sem, owns, place, real, imag)

        if results > 2:

            @pl.when(kind == 1)
            def _():
                store(stage_out, out, out_sem, outs, place, real, imag)

        return plane, side, owns + (kind == 0).astype(jnp.int32), outs + (kind == 1).astype(jnp.int32)

    zero = jnp.int32(0)
    _, _, owns, outs = lax.fori_loop(0, count, task, (zero - 1, zero + 1, zero, zero))
    settle(stage_own, own, own_sem, owns)
    if results > 2:
        settle(stage_out, out, out_sem, outs)


def add_up(base, n, h, table, own, *refs):
    recvs = refs[:len(SENDS)]
    out, mine, theirs, real, imag, image, m_sem, t_sem, o_sem = refs[len(SENDS):]
    blocks = (n // 2) * n
    full, tail, quarter = h // LANES, h % LANES, h // 2
    wide = n * h // LANES

    def written(chunk, k):
        return pltpu.make_async_copy(
            image.at[chunk, pl.ds(2 * k * h, 2 * h)].reshape(h, 2, LANES),
            out.at[pl.ds(chunk * h, h), :, pl.ds(k * LANES, LANES)],
            o_sem.at[chunk],
        )

    for b in range(blocks):
        pltpu.make_async_copy(own.at[b], mine.at[b], m_sem.at[b]).start()
        code = table[base + b]
        for k, recv in enumerate(recvs):

            @pl.when((code & 15) == k)
            def _():
                pltpu.make_async_copy(recv.at[code >> 4], theirs.at[b], t_sem.at[b]).start()

    for b in range(blocks):
        chunk, kc = b // n, b % n
        pltpu.make_async_copy(own.at[0], mine.at[b], m_sem.at[b]).wait()
        pltpu.make_async_copy(recvs[0].at[0], theirs.at[b], t_sem.at[b]).wait()
        for part, line in ((0, real), (1, imag)):
            for k in range(full):
                at = pl.ds((part * full + k) * h, h)
                line[:, kc * h + k * LANES:kc * h + (k + 1) * LANES] = mine[b, at, :] + theirs[
                    b, at, :
                ].astype(jnp.float32)
            at = pl.ds(2 * full * h, quarter)
            rest = mine[b, at, :] + theirs[b, at, :].astype(jnp.float32)
            for fold in range(2):
                lane = (2 * fold + part) * tail
                line[
                    fold * quarter:(fold + 1) * quarter, kc * h + full * LANES:(kc + 1) * h
                ] = rest[:, lane:lane + tail]
        first, last = kc * h // LANES, (kc + 1) * h // LANES
        for k in range(first, last):
            for part, line in ((0, real), (1, imag)):
                image[chunk, pl.ds(2 * k * h + part, h, stride=2), :] = line[:, k * LANES:(k + 1) * LANES]
            written(chunk, k).start()
    for chunk in range(n // 2):
        for k in range(wide):
            written(chunk, k).wait()


def tiled(mesh, h, p):
    n = mesh.shape["col"]
    half = n // 2
    pairs, source, rows, cols = route(n)
    tasks, senders, arrives = share_out(n, rows, cols)
    gap = -(-h // LANES) * LANES
    block = 2 * h * h // LANES
    events = range(len(ARRIVALS))

    names = {e: set() for e in events}
    met = {}
    for (r, j, y, e), items in tasks.items():
        for kr, _, _, _ in items:
            met[r, j, y, kr] = min(e, met.get((r, j, y, kr), e))
    for (r, j, y, e), items in tasks.items():
        for kr, kc, _, _ in items:
            names[e] |= {cols[r, j][kc]} | ({rows[r, j][kr]} if met[r, j, y, kr] == e else set())
    names = {e: sorted(v) for e, v in names.items()}
    bases, size = {}, 3
    for e in events:
        bases[e] = size
        size += 1 + max(len(v) for k, v in tasks.items() if k[3] == e)
    final = size
    size += half * n
    table = np.zeros((n, n, 2, size), np.int32)
    for r in range(n):
        for j in range(n):
            for y in range(2):
                line = table[r, j, y]
                line[:3] = r, j, 1 if r <= j else -1
                for e in events:
                    items = tasks.get((r, j, y, e), [])
                    leaving = {i[0]: -sum(x[2] for x in items if x[0] == i[0]) for i in items}
                    items = sorted(items, key=lambda i: (leaving[i[0]], i[0], -i[2], i[3]))
                    line[bases[e]] = len(items)
                    for t, (kr, kc, kind, place) in enumerate(items):
                        row = names[e].index(rows[r, j][kr]) if met[r, j, y, kr] == e else KNOWN
                        code = row | names[e].index(cols[r, j][kc]) << 6 | kind << 12 | place << 16 | kr << 24
                        line[bases[e] + 1 + t] = code
                for i in range(half):
                    for kc in range(n):
                        index, place = arrives[r, j, y, y * half + i, kc]
                        line[final + i * n + kc] = index | place << 4

    def local(velocity, panel_weight, panel_group, tile_map, group_gain):
        here = lax.axis_index("row"), lax.axis_index("col"), lax.axis_index("panel")
        line = lax.dynamic_slice(jnp.asarray(table), (*here, 0), (1, 1, 1, size)).reshape(size)
        weight, group = panel_weight[None, :], panel_group[None, :]
        have = {"own": jnp.transpose(velocity, (1, 0, 2)), "line": line}
        anywhere = pl.BlockSpec(memory_space=pl.ANY)

        def move(*given):
            for name in given:
                with jax.named_scope("move_" + name):
                    ids = [(a[0] * n + a[1], b[0] * n + b[1]) for a, b in pairs[name]]
                    have[name] = lax.ppermute(have[source[name]], ("row", "col"), ids)

        def choose(name, first, second):
            inner = jnp.logical_and(here[1] > 0, here[1] < n - 1).astype(jnp.int32)[None]
            have[name] = pl.pallas_call(
                pick,
                out_shape=jax.ShapeDtypeStruct((6, h, p), jnp.bfloat16),
                in_specs=[pl.BlockSpec(memory_space=pltpu.SMEM)] + [anywhere] * 2,
                out_specs=anywhere,
                scratch_shapes=[pltpu.VMEM((6, h, p), jnp.bfloat16), pltpu.SemaphoreType.DMA],
                compiler_params=pltpu.CompilerParams(vmem_limit_bytes=60 << 20),
                cost_estimate=pl.CostEstimate(flops=1 << 10, bytes_accessed=1 << 10, transcendentals=0),
                name="pick",
            )(inner, have[first], have[second])

        def fence(*wanted):
            keys = list(dict.fromkeys(wanted))
            have.update(zip(keys, lax.optimization_barrier(tuple(have[k] for k in keys))))

        def blocks(e):
            boxes = [i for i, x in enumerate(SENDS) if x[0] >= e][:1]
            results = ["sums", "weighed"] + [f"sent{i}" for i in boxes]
            used = [have[k] for k in names[e]]
            carried = [(k, i) for i, k in enumerate(results) if k in have]
            made = pl.pallas_call(
                functools.partial(multiply_blocks, len(carried), len(results), bases[e], len(used), h, p, gap),
                out_shape=[
                    jax.ShapeDtypeStruct((half * n, block, LANES), jnp.float32),
                    jax.ShapeDtypeStruct((n, 2 * h, 3 * p), jnp.bfloat16),
                ]
                + [jax.ShapeDtypeStruct((SENDS[i][1], block, LANES), jnp.bfloat16) for i in boxes],
                in_specs=[pl.BlockSpec(memory_space=pltpu.SMEM)] * 3
                + [pl.BlockSpec(memory_space=pltpu.VMEM)] * 2
                + [anywhere] * (len(used) + len(carried)),
                out_specs=[anywhere] * len(results),
                input_output_aliases={5 + len(used) + at: i for at, (_, i) in enumerate(carried)},
                scratch_shapes=[
                    pltpu.VMEM((2 * h, 3 * p), jnp.bfloat16),
                    pltpu.VMEM((2, 2 * h, 3 * p), jnp.bfloat16),
                    pltpu.VMEM((2, gap + h, 3 * p), jnp.bfloat16),
                    pltpu.VMEM((2, block, LANES), jnp.float32),
                    pltpu.VMEM((2, block, LANES), jnp.bfloat16),
                    pltpu.SemaphoreType.DMA,
                    pltpu.SemaphoreType.DMA((2,)),
                    pltpu.SemaphoreType.DMA,
                    pltpu.SemaphoreType.DMA((2,)),
                    pltpu.SemaphoreType.DMA((2,)),
                    pltpu.SemaphoreType.DMA((2,)),
                ],
                compiler_params=pltpu.CompilerParams(vmem_limit_bytes=60 << 20),
                cost_estimate=pl.CostEstimate(flops=1 << 20, bytes_accessed=1 << 16, transcendentals=0),
                name=f"blocks_{e}",
            )(have["line"], tile_map, group_gain, weight, group, *used, *(have[k] for k, _ in carried))
            have.update(zip(results, made))

        def exchange(i):
            ids = [((r * n + j) * 2 + y, (r * n + j) * 2 + 1 - y) for r, j, y in senders[i]]
            with jax.named_scope(f"move_sums{i}"):
                have[f"got{i}"] = lax.ppermute(have[f"sent{i}"], ("row", "col", "panel"), ids)

        move("c0", "x0", "b", "a")
        fence("own", "a", "x0", "c0", "line")
        move("xa", "ca", "d0")
        fence("b")
        choose("z", "own", "b")
        fence("b", "z", "xa", "ca", "d0")
        move("t", "xb", "cb")
        fence("cb")
        blocks(0)
        fence("sums", "sent0", "xb")
        exchange(0)
        blocks(1)
        fence("sums", "sent1", "got0", "t")
        move("e", "xt", "ct", "da", "db")
        exchange(1)
        fence("da", "db")
        blocks(2)
        fence("sums", "sent2", "ct")
        exchange(2)
        blocks(3)
        fence("sums", "sent3", "got1", "got2", "xt", "e")
        exchange(3)
        move("dt")
        blocks(4)
        fence("dt", "sums", "sent4")
        exchange(4)
        blocks(5)
        fence("sums", "sent5", "got3", "got4")
        exchange(5)
        blocks(6)
        got = [have[f"got{i}"] for i in range(len(SENDS))]
        return pl.pallas_call(
            functools.partial(add_up, final, n, h),
            out_shape=jax.ShapeDtypeStruct((half * h, 2, n * h), jnp.float32),
            in_specs=[pl.BlockSpec(memory_space=pltpu.SMEM)] + [anywhere] * (1 + len(got)),
            out_specs=anywhere,
            scratch_shapes=[
                pltpu.VMEM((half * n, block, LANES), jnp.float32),
                pltpu.VMEM((half * n, block, LANES), jnp.bfloat16),
                pltpu.VMEM((h, n * h), jnp.float32),
                pltpu.VMEM((h, n * h), jnp.float32),
                pltpu.VMEM((half, 2 * h * n * h // LANES, LANES), jnp.float32),
                pltpu.SemaphoreType.DMA((half * n,)),
                pltpu.SemaphoreType.DMA((half * n,)),
                pltpu.SemaphoreType.DMA((half,)),
            ],
            compiler_params=pltpu.CompilerParams(vmem_limit_bytes=60 << 20),
            name="add_up",
        )(have["line"], have["sums"], *got)

    return local


def contract(left_side, right_side):
    return lax.dot_general(
        left_side, right_side, (((1,), (1,)), ((), ())), preferred_element_type=jnp.float32
    )


def plain(velocity, panel_weight, panel_group, tile_map, group_gain):
    row_index, col_index = lax.axis_index("row"), lax.axis_index("col")
    rows_block = lax.all_gather(velocity, "col", axis=0, tiled=True)
    kept = jnp.where(row_index == col_index, rows_block, 0).astype(rows_block.dtype)
    cols_block = lax.psum(kept, "row")
    gains = lax.dynamic_index_in_dim(group_gain, tile_map[row_index, col_index], 1, keepdims=False)
    scale = panel_weight * gains[panel_group]
    weighted = (rows_block.astype(jnp.float32) * scale[None, None, :]).astype(jnp.bfloat16)
    width, depth = weighted.shape[0], 3 * weighted.shape[2]
    left = weighted.reshape(width, 2 * depth)
    right = cols_block.reshape(width, 2 * depth)
    sign = jnp.where(row_index <= col_index, jnp.float32(1.0), jnp.float32(-1.0))
    real = contract(left[:, :depth], right[:, :depth]) + sign * contract(left[:, depth:], right[:, depth:])
    imag = contract(left[:, depth:], right[:, :depth]) - sign * contract(left[:, :depth], right[:, depth:])
    return lax.psum_scatter(jnp.stack((real, imag), axis=1), "panel", scatter_dimension=0, tiled=True)


def solution(mesh):
    n, panels = mesh.shape["col"], mesh.shape["panel"]

    def whole(velocity, panel_weight, panel_group, tile_map, group_gain):
        h = velocity.shape[0] // (n * n)
        p = velocity.shape[2] // panels
        fits = (
            mesh.shape["row"] == n
            and n == 4
            and panels == 2
            and h % 32 == 0
            and (h % LANES) * 4 == LANES
            and (n * h) % LANES == 0
            and p % LANES == 0
        )
        return jax.shard_map(
            tiled(mesh, h, p) if fits else plain,
            mesh=mesh,
            in_specs=(P(("row", "col"), None, "panel"), P("panel"), P("panel"), P(), P()),
            out_specs=P(("row", "panel"), None, "col"),
            check_vma=False,
        )(velocity, panel_weight, panel_group, tile_map, group_gain)

    return whole
```

```python
import functools

import jax
import jax.numpy as jnp
import numpy as np
from jax import lax
from jax.experimental import pallas as pl
from jax.experimental.pallas import tpu as pltpu
from jax.sharding import PartitionSpec as P

LANES = 128
KNOWN = 32
ARRIVALS = (
    (("own", "a", "b", "x0", "c0", "ca", "cb", "d0", "xa"), 5),
    (("xb",), 6),
    (("t", "da", "db"), 3),
    (("ct",), 5),
    (("e", "xt"), 2),
    (("dt",), 3),
    ((), 16),
)
SENDS = ((0, 3), (2, 2), (3, 2), (4, 2), (5, 3))


def route(n):
    devices = [(r, j) for r in range(n) for j in range(n)]
    holds = {"own": {d: d[1] for d in devices}}
    pairs, source = {}, {}

    def add(name, operand, moves):
        pairs[name], source[name] = moves, operand
        holds[name] = {t: holds[operand][f] for f, t in moves}

    ends = [(r, j) for r, j in devices if j in (0, n - 1)]
    inner = [d for d in devices if d not in ends]
    early = [(r, j) for r, j in ends if (r + j) % 2 == 0]
    add("a", "own", [((r, j ^ 1), (r, j)) for r, j in devices])
    add("b", "own", [((r, j ^ 3), (r, j)) for r, j in inner + early])
    holds["z"] = {(r, j): j ^ 3 if (r, j) in inner else j for r, j in devices}
    add("t", "z", [((r, j ^ (1 if (r, j) in ends else 2)), (r, j)) for r, j in devices])
    del holds["z"]
    add("e", "t", [((r, j ^ 1), (r, j)) for r, j in ends if (r, j) not in early])
    rows = {d: {} for d in devices}
    cols = {d: {} for d in devices}
    for name, held in holds.items():
        for device, plane in held.items():
            assert plane not in rows[device]
            rows[device][plane] = name
    for e, name in (("0", "own"), ("a", "a"), ("b", "b"), ("t", "t")):
        for v, kind in ((0, ""), (2, "x"), (1, "c"), (3, "d")):
            parent = 2 if v == 3 else 0
            if v:
                pairs[kind + e] = [((c ^ parent, c), (c ^ v, c)) for c in range(n)]
                source[kind + e] = "x" + e if parent else name
            for c in range(n):
                cols[c ^ v, c][holds[name][c, c]] = kind + e if v else name
    assert all(len(x) == n for d in devices for x in (rows[d], cols[d]))
    return pairs, source, rows, cols


def share_out(n, rows, cols):
    half = n // 2
    event = {name: e for e, (names, _) in enumerate(ARRIVALS) for name in names}
    window = [min((i for i, x in enumerate(SENDS) if x[0] >= e), default=None) for e in range(len(ARRIVALS))]
    tasks, senders, arrives = {}, [[] for _ in SENDS], {}

    def attempt(blocks, chosen):
        wait, plan = list(blocks), []
        room = [x[1] if i in chosen else 0 for i, x in enumerate(SENDS)]
        for e, (_, most) in enumerate(ARRIVALS):
            i = window[e]
            now = [b for b in wait if b[0] <= e]
            leave = [] if i is None else [b for b in now if not b[1]][:min(most, room[i])]
            if leave:
                room[i] -= len(leave)
            stay = [b for b in now if b[1]][:most - len(leave)]
            for b in leave + stay:
                wait.remove(b)
                plan.append((e, i if b in leave else None, b[2], b[3]))
        return None if wait else plan

    for r in range(n):
        for j in range(n):
            for y in range(2):
                blocks = sorted(
                    (max(event[rows[r, j][kr]], event[cols[r, j][kc]]), kr // half == y, kr, kc)
                    for kr in range(n)
                    for kc in range(n)
                )
                best = None
                for mask in range(1 << len(SENDS)):
                    chosen = [i for i in range(len(SENDS)) if mask >> i & 1]
                    plan = attempt(blocks, chosen)
                    if plan is None:
                        continue
                    cost = sum(SENDS[i][1] * i**2 for i in chosen), sum(e * e for e, _, _, _ in plan)
                    if best is None or cost < best[0]:
                        best = cost, plan
                used = {}
                for e, i, kr, kc in best[1]:
                    if i is None:
                        place = (kr - y * half) * n + kc
                    else:
                        place = used[i] = used.get(i, -1) + 1
                        arrives[r, j, 1 - y, kr, kc] = i, place
                    tasks.setdefault((r, j, y, e), []).append((kr, kc, int(i is not None), place))
                for i in used:
                    senders[i].append((r, j, y))
    return tasks, senders, arrives


def rate(w_ref, group_ref, gain_ref, region):
    groups = group_ref[...]
    gain = jnp.zeros(groups.shape, jnp.float32)
    for g in range(gain_ref.shape[0]):
        gain = gain + jnp.where(groups == g, gain_ref[g, region], jnp.float32(0.0))
    return w_ref[...] * gain


def fetch(index, sources, target, sem, h, p, gap):
    for i, source in enumerate(sources):

        @pl.when(index == i)
        def _():
            for c in range(6):
                pltpu.make_async_copy(
                    source.at[c], target.at[pl.ds((c // 3) * gap, h), pl.ds((c % 3) * p, p)], sem
                ).start()


def landed(sources, target, sem, h, p, gap):
    for c in range(6):
        pltpu.make_async_copy(
            sources[0].at[c], target.at[pl.ds((c // 3) * gap, h), pl.ds((c % 3) * p, p)], sem
        ).wait()


def pack(stage, real, imag, h):
    tail, quarter = h % LANES, h // 2
    full = h // LANES
    for part, value in ((0, real), (1, imag)):
        for k in range(full):
            stage[pl.ds((part * full + k) * h, h), :] = value[:, k * LANES:(k + 1) * LANES].astype(stage.dtype)
        for fold in range(2):
            lane = (2 * fold + part) * tail
            stage[pl.ds(2 * full * h, quarter), lane:lane + tail] = value[
                fold * quarter:(fold + 1) * quarter, full * LANES:
            ].astype(stage.dtype)


def pick(second, first_ref, second_ref, out, held, sem):
    for k, source in enumerate((first_ref, second_ref)):

        @pl.when(second[0] == k)
        def _():
            pltpu.make_async_copy(source, held, sem).start()

    pltpu.make_async_copy(first_ref, held, sem).wait()
    copy = pltpu.make_async_copy(held, out, sem)
    copy.start()
    copy.wait()


def multiply_blocks(passed, results, base, sources, h, p, gap, table, tile_map, gain_ref, w_ref, group_ref, *refs):
    srcs = refs[:sources]
    refs = refs[sources + passed:]
    own, weighed, out = refs[0], refs[1], refs[results - 1]
    raw, left, right, stage_own, stage_out, raw_sem, l_sem, w_sem, r_sem, own_sem, out_sem = refs[results:]
    count = table[base]
    sign = table[2].astype(jnp.float32)
    scale = rate(w_ref, group_ref, gain_ref, tile_map[table[0], table[1]])

    def entry(t):
        code = table[base + 1 + t]
        return code & 63, (code >> 6) & 63, (code >> 12) & 15, (code >> 16) & 255, code >> 24

    def stored(stage, target, sem, slot, place):
        return pltpu.make_async_copy(stage.at[slot], target.at[place], sem.at[slot])

    def store(stage, target, sem, done, place, real, imag):
        slot = lax.rem(done, 2)

        @pl.when(done > 1)
        def _():
            stored(stage, target, sem, slot, 0).wait()

        pack(stage.at[slot], real, imag, h)
        stored(stage, target, sem, slot, place).start()

    def settle(stage, target, sem, done):
        for back in (1, 2):

            @pl.when(done >= back)
            def _():
                stored(stage, target, sem, lax.rem(done - back, 2), 0).wait()

    def known(slot, plane):
        return pltpu.make_async_copy(weighed.at[plane], left.at[slot], l_sem.at[slot])

    def kept(slot, plane):
        return pltpu.make_async_copy(left.at[slot], weighed.at[plane], w_sem)

    def ask_row(t, slot):
        row, plane = entry(t)[0], entry(t)[4]
        fetch(row, srcs, raw, raw_sem, h, p, h)

        @pl.when(row >= KNOWN)
        def _():
            known(slot, plane).start()

    def ask_column(t):
        fetch(entry(t)[1], srcs, right.at[lax.rem(t, 2)], r_sem.at[lax.rem(t, 2)], h, p, gap)

    @pl.when(count > 0)
    def _():
        ask_row(0, 0)
        ask_column(0)

    def task(t, carry):
        before, side, owns, outs = carry
        row, _, kind, place, plane = entry(t)
        slot = lax.rem(t, 2)
        changed = plane != before
        side = jnp.where(changed, 1 - side, side)
        fresh = jnp.logical_and(changed, row < KNOWN)

        @pl.when(jnp.logical_and(changed, row >= KNOWN))
        def _():
            known(side, plane).wait()

        @pl.when(fresh)
        def _():
            landed(srcs, raw, raw_sem, h, p, h)
            for c in range(3):
                part = raw[:, c * p:(c + 1) * p].astype(jnp.float32)
                left[side, :, c * p:(c + 1) * p] = (part * scale).astype(jnp.bfloat16)
            kept(side, plane).start()

        @pl.when(t + 1 < count)
        def _():
            ask_column(t + 1)

            @pl.when(entry(t + 1)[4] != plane)
            def _():
                ask_row(t + 1, 1 - side)

        landed(srcs, right.at[slot], r_sem.at[slot], h, p, gap)
        product = lax.dot_general(
            left[side], right[slot], (((1,), (1,)), ((), ())), preferred_element_type=jnp.float32
        )
        real = product[:h, :h] + sign * product[h:, gap:gap + h]
        imag = product[h:, :h] - sign * product[:h, gap:gap + h]

        @pl.when(fresh)
        def _():
            kept(side, plane).wait()

        @pl.when(kind == 0)
        def _():
            store(stage_own, own, own_sem, owns, place, real, imag)

        if results > 2:

            @pl.when(kind == 1)
            def _():
                store(stage_out, out, out_sem, outs, place, real, imag)

        return plane, side, owns + (kind == 0).astype(jnp.int32), outs + (kind == 1).astype(jnp.int32)

    zero = jnp.int32(0)
    _, _, owns, outs = lax.fori_loop(0, count, task, (zero - 1, zero + 1, zero, zero))
    settle(stage_own, own, own_sem, owns)
    if results > 2:
        settle(stage_out, out, out_sem, outs)


def add_up(base, n, h, table, own, *refs):
    recvs = refs[:len(SENDS)]
    out, mine, theirs, real, imag, image, m_sem, t_sem, o_sem = refs[len(SENDS):]
    blocks = (n // 2) * n
    full, tail, quarter = h // LANES, h % LANES, h // 2
    wide = n * h // LANES

    def written(chunk, k):
        return pltpu.make_async_copy(
            image.at[chunk, pl.ds(2 * k * h, 2 * h)].reshape(h, 2, LANES),
            out.at[pl.ds(chunk * h, h), :, pl.ds(k * LANES, LANES)],
            o_sem.at[chunk],
        )

    for b in range(blocks):
        pltpu.make_async_copy(own.at[b], mine.at[b], m_sem.at[b]).start()
        code = table[base + b]
        for k, recv in enumerate(recvs):

            @pl.when((code & 15) == k)
            def _():
                pltpu.make_async_copy(recv.at[code >> 4], theirs.at[b], t_sem.at[b]).start()

    for b in range(blocks):
        chunk, kc = b // n, b % n
        pltpu.make_async_copy(own.at[0], mine.at[b], m_sem.at[b]).wait()
        pltpu.make_async_copy(recvs[0].at[0], theirs.at[b], t_sem.at[b]).wait()
        for part, line in ((0, real), (1, imag)):
            for k in range(full):
                at = pl.ds((part * full + k) * h, h)
                line[:, kc * h + k * LANES:kc * h + (k + 1) * LANES] = mine[b, at, :] + theirs[
                    b, at, :
                ].astype(jnp.float32)
            at = pl.ds(2 * full * h, quarter)
            rest = mine[b, at, :] + theirs[b, at, :].astype(jnp.float32)
            for fold in range(2):
                lane = (2 * fold + part) * tail
                line[
                    fold * quarter:(fold + 1) * quarter, kc * h + full * LANES:(kc + 1) * h
                ] = rest[:, lane:lane + tail]
        first, last = kc * h // LANES, (kc + 1) * h // LANES
        for k in range(first, last):
            for part, line in ((0, real), (1, imag)):
                image[chunk, pl.ds(2 * k * h + part, h, stride=2), :] = line[:, k * LANES:(k + 1) * LANES]
            written(chunk, k).start()
    for chunk in range(n // 2):
        for k in range(wide):
            written(chunk, k).wait()


def tiled(mesh, h, p):
    n = mesh.shape["col"]
    half = n // 2
    pairs, source, rows, cols = route(n)
    tasks, senders, arrives = share_out(n, rows, cols)
    gap = -(-h // LANES) * LANES
    block = 2 * h * h // LANES
    events = range(len(ARRIVALS))

    names = {e: set() for e in events}
    met = {}
    for (r, j, y, e), items in tasks.items():
        for kr, _, _, _ in items:
            met[r, j, y, kr] = min(e, met.get((r, j, y, kr), e))
    for (r, j, y, e), items in tasks.items():
        for kr, kc, _, _ in items:
            names[e] |= {cols[r, j][kc]} | ({rows[r, j][kr]} if met[r, j, y, kr] == e else set())
    names = {e: sorted(v) for e, v in names.items()}
    bases, size = {}, 3
    for e in events:
        bases[e] = size
        size += 1 + max(len(v) for k, v in tasks.items() if k[3] == e)
    final = size
    size += half * n
    table = np.zeros((n, n, 2, size), np.int32)
    for r in range(n):
        for j in range(n):
            for y in range(2):
                line = table[r, j, y]
                line[:3] = r, j, 1 if r <= j else -1
                for e in events:
                    items = tasks.get((r, j, y, e), [])
                    leaving = {i[0]: -sum(x[2] for x in items if x[0] == i[0]) for i in items}
                    items = sorted(items, key=lambda i: (leaving[i[0]], i[0], -i[2], i[3]))
                    line[bases[e]] = len(items)
                    for t, (kr, kc, kind, place) in enumerate(items):
                        row = names[e].index(rows[r, j][kr]) if met[r, j, y, kr] == e else KNOWN
                        code = row | names[e].index(cols[r, j][kc]) << 6 | kind << 12 | place << 16 | kr << 24
                        line[bases[e] + 1 + t] = code
                for i in range(half):
                    for kc in range(n):
                        index, place = arrives[r, j, y, y * half + i, kc]
                        line[final + i * n + kc] = index | place << 4

    def local(velocity, panel_weight, panel_group, tile_map, group_gain):
        here = lax.axis_index("row"), lax.axis_index("col"), lax.axis_index("panel")
        line = lax.dynamic_slice(jnp.asarray(table), (*here, 0), (1, 1, 1, size)).reshape(size)
        weight, group = panel_weight[None, :], panel_group[None, :]
        have = {"own": jnp.transpose(velocity, (1, 0, 2)), "line": line}
        anywhere = pl.BlockSpec(memory_space=pl.ANY)

        def move(*given):
            for name in given:
                with jax.named_scope("move_" + name):
                    ids = [(a[0] * n + a[1], b[0] * n + b[1]) for a, b in pairs[name]]
                    have[name] = lax.ppermute(have[source[name]], ("row", "col"), ids)

        def choose(name, first, second):
            inner = jnp.logical_and(here[1] > 0, here[1] < n - 1).astype(jnp.int32)[None]
            have[name] = pl.pallas_call(
                pick,
                out_shape=jax.ShapeDtypeStruct((6, h, p), jnp.bfloat16),
                in_specs=[pl.BlockSpec(memory_space=pltpu.SMEM)] + [anywhere] * 2,
                out_specs=anywhere,
                scratch_shapes=[pltpu.VMEM((6, h, p), jnp.bfloat16), pltpu.SemaphoreType.DMA],
                compiler_params=pltpu.CompilerParams(vmem_limit_bytes=64 << 20),
                cost_estimate=pl.CostEstimate(flops=1 << 10, bytes_accessed=1 << 10, transcendentals=0),
                name="pick",
            )(inner, have[first], have[second])

        def fence(*wanted):
            keys = list(dict.fromkeys(wanted))
            have.update(zip(keys, lax.optimization_barrier(tuple(have[k] for k in keys))))

        def blocks(e):
            boxes = [i for i, x in enumerate(SENDS) if x[0] >= e][:1]
            results = ["sums", "weighed"] + [f"sent{i}" for i in boxes]
            used = [have[k] for k in names[e]]
            carried = [(k, i) for i, k in enumerate(results) if k in have]
            made = pl.pallas_call(
                functools.partial(multiply_blocks, len(carried), len(results), bases[e], len(used), h, p, gap),
                out_shape=[
                    jax.ShapeDtypeStruct((half * n, block, LANES), jnp.float32),
                    jax.ShapeDtypeStruct((n, 2 * h, 3 * p), jnp.bfloat16),
                ]
                + [jax.ShapeDtypeStruct((SENDS[i][1], block, LANES), jnp.bfloat16) for i in boxes],
                in_specs=[pl.BlockSpec(memory_space=pltpu.SMEM)] * 3
                + [pl.BlockSpec(memory_space=pltpu.VMEM)] * 2
                + [anywhere] * (len(used) + len(carried)),
                out_specs=[anywhere] * len(results),
                input_output_aliases={5 + len(used) + at: i for at, (_, i) in enumerate(carried)},
                scratch_shapes=[
                    pltpu.VMEM((2 * h, 3 * p), jnp.bfloat16),
                    pltpu.VMEM((2, 2 * h, 3 * p), jnp.bfloat16),
                    pltpu.VMEM((2, gap + h, 3 * p), jnp.bfloat16),
                    pltpu.VMEM((2, block, LANES), jnp.float32),
                    pltpu.VMEM((2, block, LANES), jnp.bfloat16),
                    pltpu.SemaphoreType.DMA,
                    pltpu.SemaphoreType.DMA((2,)),
                    pltpu.SemaphoreType.DMA,
                    pltpu.SemaphoreType.DMA((2,)),
                    pltpu.SemaphoreType.DMA((2,)),
                    pltpu.SemaphoreType.DMA((2,)),
                ],
                compiler_params=pltpu.CompilerParams(vmem_limit_bytes=64 << 20),
                cost_estimate=pl.CostEstimate(flops=1 << 20, bytes_accessed=1 << 16, transcendentals=0),
                name=f"blocks_{e}",
            )(have["line"], tile_map, group_gain, weight, group, *used, *(have[k] for k, _ in carried))
            have.update(zip(results, made))

        def exchange(i):
            ids = [((r * n + j) * 2 + y, (r * n + j) * 2 + 1 - y) for r, j, y in senders[i]]
            with jax.named_scope(f"move_sums{i}"):
                have[f"got{i}"] = lax.ppermute(have[f"sent{i}"], ("row", "col", "panel"), ids)

        move("c0", "x0", "b", "a")
        fence("own", "a", "x0", "c0", "line")
        move("xa", "ca", "d0")
        fence("b")
        choose("z", "own", "b")
        fence("b", "z", "xa", "ca", "d0")
        move("t", "xb", "cb")
        fence("cb")
        blocks(0)
        fence("sums", "sent0", "xb")
        exchange(0)
        blocks(1)
        fence("sums", "sent1", "got0", "t")
        move("e", "xt", "ct", "da", "db")
        fence("da", "db")
        blocks(2)
        fence("sums", "sent1", "ct")
        exchange(1)
        blocks(3)
        fence("sums", "sent2", "got1", "xt", "e")
        exchange(2)
        move("dt")
        blocks(4)
        fence("dt", "sums", "sent3")
        exchange(3)
        blocks(5)
        fence("sums", "sent4", "got2", "got3")
        exchange(4)
        blocks(6)
        got = [have[f"got{i}"] for i in range(len(SENDS))]
        return pl.pallas_call(
            functools.partial(add_up, final, n, h),
            out_shape=jax.ShapeDtypeStruct((half * h, 2, n * h), jnp.float32),
            in_specs=[pl.BlockSpec(memory_space=pltpu.SMEM)] + [anywhere] * (1 + len(got)),
            out_specs=anywhere,
            scratch_shapes=[
                pltpu.VMEM((half * n, block, LANES), jnp.float32),
                pltpu.VMEM((half * n, block, LANES), jnp.bfloat16),
                pltpu.VMEM((h, n * h), jnp.float32),
                pltpu.VMEM((h, n * h), jnp.float32),
                pltpu.VMEM((half, 2 * h * n * h // LANES, LANES), jnp.float32),
                pltpu.SemaphoreType.DMA((half * n,)),
                pltpu.SemaphoreType.DMA((half * n,)),
                pltpu.SemaphoreType.DMA((half,)),
            ],
            compiler_params=pltpu.CompilerParams(vmem_limit_bytes=64 << 20),
            name="add_up",
        )(have["line"], have["sums"], *got)

    return local


def contract(left_side, right_side):
    return lax.dot_general(
        left_side, right_side, (((1,), (1,)), ((), ())), preferred_element_type=jnp.float32
    )


def plain(velocity, panel_weight, panel_group, tile_map, group_gain):
    row_index, col_index = lax.axis_index("row"), lax.axis_index("col")
    rows_block = lax.all_gather(velocity, "col", axis=0, tiled=True)
    kept = jnp.where(row_index == col_index, rows_block, 0).astype(rows_block.dtype)
    cols_block = lax.psum(kept, "row")
    gains = lax.dynamic_index_in_dim(group_gain, tile_map[row_index, col_index], 1, keepdims=False)
    scale = panel_weight * gains[panel_group]
    weighted = (rows_block.astype(jnp.float32) * scale[None, None, :]).astype(jnp.bfloat16)
    width, depth = weighted.shape[0], 3 * weighted.shape[2]
    left = weighted.reshape(width, 2 * depth)
    right = cols_block.reshape(width, 2 * depth)
    sign = jnp.where(row_index <= col_index, jnp.float32(1.0), jnp.float32(-1.0))
    real = contract(left[:, :depth], right[:, :depth]) + sign * contract(left[:, depth:], right[:, depth:])
    imag = contract(left[:, depth:], right[:, :depth]) - sign * contract(left[:, :depth], right[:, depth:])
    return lax.psum_scatter(jnp.stack((real, imag), axis=1), "panel", scatter_dimension=0, tiled=True)


def solution(mesh):
    n, panels = mesh.shape["col"], mesh.shape["panel"]

    def whole(velocity, panel_weight, panel_group, tile_map, group_gain):
        h = velocity.shape[0] // (n * n)
        p = velocity.shape[2] // panels
        fits = (
            mesh.shape["row"] == n
            and n == 4
            and panels == 2
            and h % 32 == 0
            and (h % LANES) * 4 == LANES
            and (n * h) % LANES == 0
            and p % LANES == 0
        )
        return jax.shard_map(
            tiled(mesh, h, p) if fits else plain,
            mesh=mesh,
            in_specs=(P(("row", "col"), None, "panel"), P("panel"), P("panel"), P(), P()),
            out_specs=P(("row", "panel"), None, "col"),
            check_vma=False,
        )(velocity, panel_weight, panel_group, tile_map, group_gain)

    return whole
```

```python
import functools

import jax
import jax.numpy as jnp
import numpy as np
from jax import lax
from jax.experimental import pallas as pl
from jax.experimental.pallas import tpu as pltpu
from jax.sharding import PartitionSpec as P

LANES = 128
KNOWN = 32
ARRIVALS = (
    (("own", "a", "b", "x0", "c0", "ca", "cb", "d0", "xa"), 5),
    (("xb",), 6),
    (("t", "da", "db"), 3),
    (("ct",), 5),
    (("e", "xt"), 2),
    (("dt",), 3),
    ((), 16),
)
SENDS = ((0, 3), (2, 2), (3, 2), (4, 2), (5, 3))


def route(n):
    devices = [(r, j) for r in range(n) for j in range(n)]
    holds = {"own": {d: d[1] for d in devices}}
    pairs, source = {}, {}

    def add(name, operand, moves):
        pairs[name], source[name] = moves, operand
        holds[name] = {t: holds[operand][f] for f, t in moves}

    ends = [(r, j) for r, j in devices if j in (0, n - 1)]
    inner = [d for d in devices if d not in ends]
    early = [(r, j) for r, j in ends if (r + j) % 2 == 0]
    add("a", "own", [((r, j ^ 1), (r, j)) for r, j in devices])
    add("b", "own", [((r, j ^ 3), (r, j)) for r, j in inner + early])
    holds["z"] = {(r, j): j ^ 3 if (r, j) in inner else j for r, j in devices}
    add("t", "z", [((r, j ^ (1 if (r, j) in ends else 2)), (r, j)) for r, j in devices])
    del holds["z"]
    add("e", "t", [((r, j ^ 1), (r, j)) for r, j in ends if (r, j) not in early])
    rows = {d: {} for d in devices}
    cols = {d: {} for d in devices}
    for name, held in holds.items():
        for device, plane in held.items():
            assert plane not in rows[device]
            rows[device][plane] = name
    for e, name in (("0", "own"), ("a", "a"), ("b", "b"), ("t", "t")):
        for v, kind in ((0, ""), (2, "x"), (1, "c"), (3, "d")):
            parent = 2 if v == 3 else 0
            if v:
                pairs[kind + e] = [((c ^ parent, c), (c ^ v, c)) for c in range(n)]
                source[kind + e] = "x" + e if parent else name
            for c in range(n):
                cols[c ^ v, c][holds[name][c, c]] = kind + e if v else name
    assert all(len(x) == n for d in devices for x in (rows[d], cols[d]))
    return pairs, source, rows, cols


def share_out(n, rows, cols):
    half = n // 2
    event = {name: e for e, (names, _) in enumerate(ARRIVALS) for name in names}
    window = [min((i for i, x in enumerate(SENDS) if x[0] >= e), default=None) for e in range(len(ARRIVALS))]
    tasks, senders, arrives = {}, [[] for _ in SENDS], {}

    def attempt(blocks, chosen):
        wait, plan = list(blocks), []
        room = [x[1] if i in chosen else 0 for i, x in enumerate(SENDS)]
        for e, (_, most) in enumerate(ARRIVALS):
            i = window[e]
            now = [b for b in wait if b[0] <= e]
            leave = [] if i is None else [b for b in now if not b[1]][:min(most, room[i])]
            if leave:
                room[i] -= len(leave)
            stay = [b for b in now if b[1]][:most - len(leave)]
            for b in leave + stay:
                wait.remove(b)
                plan.append((e, i if b in leave else None, b[2], b[3]))
        return None if wait else plan

    for r in range(n):
        for j in range(n):
            for y in range(2):
                blocks = sorted(
                    (max(event[rows[r, j][kr]], event[cols[r, j][kc]]), kr // half == y, kr, kc)
                    for kr in range(n)
                    for kc in range(n)
                )
                best = None
                for mask in range(1 << len(SENDS)):
                    chosen = [i for i in range(len(SENDS)) if mask >> i & 1]
                    plan = attempt(blocks, chosen)
                    if plan is None:
                        continue
                    cost = sum(SENDS[i][1] * i**2 for i in chosen), sum(e * e for e, _, _, _ in plan)
                    if best is None or cost < best[0]:
                        best = cost, plan
                used = {}
                for e, i, kr, kc in best[1]:
                    if i is None:
                        place = (kr - y * half) * n + kc
                    else:
                        place = used[i] = used.get(i, -1) + 1
                        arrives[r, j, 1 - y, kr, kc] = i, place
                    tasks.setdefault((r, j, y, e), []).append((kr, kc, int(i is not None), place))
                for i in used:
                    senders[i].append((r, j, y))
    return tasks, senders, arrives


def rate(w_ref, group_ref, gain_ref, region):
    groups = group_ref[...]
    gain = jnp.zeros(groups.shape, jnp.float32)
    for g in range(gain_ref.shape[0]):
        gain = gain + jnp.where(groups == g, gain_ref[g, region], jnp.float32(0.0))
    return w_ref[...] * gain


def fetch(index, sources, target, sem, h, p, gap):
    for i, source in enumerate(sources):

        @pl.when(index == i)
        def _():
            for c in range(6):
                pltpu.make_async_copy(
                    source.at[c], target.at[pl.ds((c // 3) * gap, h), pl.ds((c % 3) * p, p)], sem
                ).start()


def landed(sources, target, sem, h, p, gap):
    for c in range(6):
        pltpu.make_async_copy(
            sources[0].at[c], target.at[pl.ds((c // 3) * gap, h), pl.ds((c % 3) * p, p)], sem
        ).wait()


def pack(stage, real, imag, h):
    tail, quarter = h % LANES, h // 2
    full = h // LANES
    for part, value in ((0, real), (1, imag)):
        for k in range(full):
            stage[pl.ds((part * full + k) * h, h), :] = value[:, k * LANES:(k + 1) * LANES].astype(stage.dtype)
        for fold in range(2):
            lane = (2 * fold + part) * tail
            stage[pl.ds(2 * full * h, quarter), lane:lane + tail] = value[
                fold * quarter:(fold + 1) * quarter, full * LANES:
            ].astype(stage.dtype)


def pick(second, first_ref, second_ref, out, held, sem):
    for k, source in enumerate((first_ref, second_ref)):

        @pl.when(second[0] == k)
        def _():
            pltpu.make_async_copy(source, held, sem).start()

    pltpu.make_async_copy(first_ref, held, sem).wait()
    copy = pltpu.make_async_copy(held, out, sem)
    copy.start()
    copy.wait()


def multiply_blocks(passed, results, base, sources, h, p, gap, table, tile_map, gain_ref, w_ref, group_ref, *refs):
    srcs = refs[:sources]
    refs = refs[sources + passed:]
    own, weighed, out = refs[0], refs[1], refs[results - 1]
    raw, left, right, stage_own, stage_out, raw_sem, l_sem, w_sem, r_sem, own_sem, out_sem = refs[results:]
    count = table[base]
    sign = table[2].astype(jnp.float32)
    scale = rate(w_ref, group_ref, gain_ref, tile_map[table[0], table[1]])

    def entry(t):
        code = table[base + 1 + t]
        return code & 63, (code >> 6) & 63, (code >> 12) & 15, (code >> 16) & 255, code >> 24

    def stored(stage, target, sem, slot, place):
        return pltpu.make_async_copy(stage.at[slot], target.at[place], sem.at[slot])

    def store(stage, target, sem, done, place, real, imag):
        slot = lax.rem(done, 2)

        @pl.when(done > 1)
        def _():
            stored(stage, target, sem, slot, 0).wait()

        pack(stage.at[slot], real, imag, h)
        stored(stage, target, sem, slot, place).start()

    def settle(stage, target, sem, done):
        for back in (1, 2):

            @pl.when(done >= back)
            def _():
                stored(stage, target, sem, lax.rem(done - back, 2), 0).wait()

    def known(slot, plane):
        return pltpu.make_async_copy(weighed.at[plane], left.at[slot], l_sem.at[slot])

    def kept(slot, plane):
        return pltpu.make_async_copy(left.at[slot], weighed.at[plane], w_sem)

    def ask_row(t, slot):
        row, plane = entry(t)[0], entry(t)[4]
        fetch(row, srcs, raw, raw_sem, h, p, h)

        @pl.when(row >= KNOWN)
        def _():
            known(slot, plane).start()

    def ask_column(t):
        fetch(entry(t)[1], srcs, right.at[lax.rem(t, 2)], r_sem.at[lax.rem(t, 2)], h, p, gap)

    @pl.when(count > 0)
    def _():
        ask_row(0, 0)
        ask_column(0)

    def task(t, carry):
        before, side, owns, outs = carry
        row, _, kind, place, plane = entry(t)
        slot = lax.rem(t, 2)
        changed = plane != before
        side = jnp.where(changed, 1 - side, side)
        fresh = jnp.logical_and(changed, row < KNOWN)

        @pl.when(jnp.logical_and(changed, row >= KNOWN))
        def _():
            known(side, plane).wait()

        @pl.when(fresh)
        def _():
            landed(srcs, raw, raw_sem, h, p, h)
            for c in range(3):
                part = raw[:, c * p:(c + 1) * p].astype(jnp.float32)
                left[side, :, c * p:(c + 1) * p] = (part * scale).astype(jnp.bfloat16)
            kept(side, plane).start()

        @pl.when(t + 1 < count)
        def _():
            ask_column(t + 1)

            @pl.when(entry(t + 1)[4] != plane)
            def _():
                ask_row(t + 1, 1 - side)

        landed(srcs, right.at[slot], r_sem.at[slot], h, p, gap)
        product = lax.dot_general(
            left[side], right[slot], (((1,), (1,)), ((), ())), preferred_element_type=jnp.float32
        )
        real = product[:h, :h] + sign * product[h:, gap:gap + h]
        imag = product[h:, :h] - sign * product[:h, gap:gap + h]

        @pl.when(fresh)
        def _():
            kept(side, plane).wait()

        @pl.when(kind == 0)
        def _():
            store(stage_own, own, own_sem, owns, place, real, imag)

        if results > 2:

            @pl.when(kind == 1)
            def _():
                store(stage_out, out, out_sem, outs, place, real, imag)

        return plane, side, owns + (kind == 0).astype(jnp.int32), outs + (kind == 1).astype(jnp.int32)

    zero = jnp.int32(0)
    _, _, owns, outs = lax.fori_loop(0, count, task, (zero - 1, zero + 1, zero, zero))
    settle(stage_own, own, own_sem, owns)
    if results > 2:
        settle(stage_out, out, out_sem, outs)


def add_up(base, n, h, table, own, *refs):
    recvs = refs[:len(SENDS)]
    out, mine, theirs, real, imag, image, m_sem, t_sem, o_sem = refs[len(SENDS):]
    blocks = (n // 2) * n
    full, tail, quarter = h // LANES, h % LANES, h // 2
    wide = n * h // LANES

    def written(chunk, k):
        return pltpu.make_async_copy(
            image.at[chunk, pl.ds(2 * k * h, 2 * h)].reshape(h, 2, LANES),
            out.at[pl.ds(chunk * h, h), :, pl.ds(k * LANES, LANES)],
            o_sem.at[chunk],
        )

    for b in range(blocks):
        pltpu.make_async_copy(own.at[b], mine.at[b], m_sem.at[b]).start()
        code = table[base + b]
        for k, recv in enumerate(recvs):

            @pl.when((code & 15) == k)
            def _():
                pltpu.make_async_copy(recv.at[code >> 4], theirs.at[b], t_sem.at[b]).start()

    for b in range(blocks):
        chunk, kc = b // n, b % n
        pltpu.make_async_copy(own.at[0], mine.at[b], m_sem.at[b]).wait()
        pltpu.make_async_copy(recvs[0].at[0], theirs.at[b], t_sem.at[b]).wait()
        for part, line in ((0, real), (1, imag)):
            for k in range(full):
                at = pl.ds((part * full + k) * h, h)
                line[:, kc * h + k * LANES:kc * h + (k + 1) * LANES] = mine[b, at, :] + theirs[
                    b, at, :
                ].astype(jnp.float32)
            at = pl.ds(2 * full * h, quarter)
            rest = mine[b, at, :] + theirs[b, at, :].astype(jnp.float32)
            for fold in range(2):
                lane = (2 * fold + part) * tail
                line[
                    fold * quarter:(fold + 1) * quarter, kc * h + full * LANES:(kc + 1) * h
                ] = rest[:, lane:lane + tail]
        first, last = kc * h // LANES, (kc + 1) * h // LANES
        for k in range(first, last):
            for part, line in ((0, real), (1, imag)):
                image[chunk, pl.ds(2 * k * h + part, h, stride=2), :] = line[:, k * LANES:(k + 1) * LANES]
            written(chunk, k).start()
    for chunk in range(n // 2):
        for k in range(wide):
            written(chunk, k).wait()


def tiled(mesh, h, p):
    n = mesh.shape["col"]
    half = n // 2
    pairs, source, rows, cols = route(n)
    tasks, senders, arrives = share_out(n, rows, cols)
    gap = -(-h // LANES) * LANES
    block = 2 * h * h // LANES
    events = range(len(ARRIVALS))

    names = {e: set() for e in events}
    met = {}
    for (r, j, y, e), items in tasks.items():
        for kr, _, _, _ in items:
            met[r, j, y, kr] = min(e, met.get((r, j, y, kr), e))
    for (r, j, y, e), items in tasks.items():
        for kr, kc, _, _ in items:
            names[e] |= {cols[r, j][kc]} | ({rows[r, j][kr]} if met[r, j, y, kr] == e else set())
    names = {e: sorted(v) for e, v in names.items()}
    bases, size = {}, 3
    for e in events:
        bases[e] = size
        size += 1 + max(len(v) for k, v in tasks.items() if k[3] == e)
    final = size
    size += half * n
    table = np.zeros((n, n, 2, size), np.int32)
    for r in range(n):
        for j in range(n):
            for y in range(2):
                line = table[r, j, y]
                line[:3] = r, j, 1 if r <= j else -1
                for e in events:
                    items = tasks.get((r, j, y, e), [])
                    leaving = {i[0]: -sum(x[2] for x in items if x[0] == i[0]) for i in items}
                    items = sorted(items, key=lambda i: (leaving[i[0]], i[0], -i[2], i[3]))
                    line[bases[e]] = len(items)
                    for t, (kr, kc, kind, place) in enumerate(items):
                        row = names[e].index(rows[r, j][kr]) if met[r, j, y, kr] == e else KNOWN
                        code = row | names[e].index(cols[r, j][kc]) << 6 | kind << 12 | place << 16 | kr << 24
                        line[bases[e] + 1 + t] = code
                for i in range(half):
                    for kc in range(n):
                        index, place = arrives[r, j, y, y * half + i, kc]
                        line[final + i * n + kc] = index | place << 4

    def local(velocity, panel_weight, panel_group, tile_map, group_gain):
        here = lax.axis_index("row"), lax.axis_index("col"), lax.axis_index("panel")
        line = lax.dynamic_slice(jnp.asarray(table), (*here, 0), (1, 1, 1, size)).reshape(size)
        weight, group = panel_weight[None, :], panel_group[None, :]
        have = {"own": jnp.transpose(velocity, (1, 0, 2)), "line": line}
        anywhere = pl.BlockSpec(memory_space=pl.ANY)

        def move(*given):
            for name in given:
                with jax.named_scope("move_" + name):
                    ids = [(a[0] * n + a[1], b[0] * n + b[1]) for a, b in pairs[name]]
                    have[name] = lax.ppermute(have[source[name]], ("row", "col"), ids)

        def choose(name, first, second):
            inner = jnp.logical_and(here[1] > 0, here[1] < n - 1).astype(jnp.int32)[None]
            have[name] = pl.pallas_call(
                pick,
                out_shape=jax.ShapeDtypeStruct((6, h, p), jnp.bfloat16),
                in_specs=[pl.BlockSpec(memory_space=pltpu.SMEM)] + [anywhere] * 2,
                out_specs=anywhere,
                scratch_shapes=[pltpu.VMEM((6, h, p), jnp.bfloat16), pltpu.SemaphoreType.DMA],
                compiler_params=pltpu.CompilerParams(vmem_limit_bytes=64 << 20),
                cost_estimate=pl.CostEstimate(flops=1 << 10, bytes_accessed=1 << 10, transcendentals=0),
                name="pick",
            )(inner, have[first], have[second])

        def fence(*wanted):
            keys = list(dict.fromkeys(wanted))
            have.update(zip(keys, lax.optimization_barrier(tuple(have[k] for k in keys))))

        def blocks(e):
            boxes = [i for i, x in enumerate(SENDS) if x[0] >= e][:1]
            results = ["sums", "weighed"] + [f"sent{i}" for i in boxes]
            used = [have[k] for k in names[e]]
            carried = [(k, i) for i, k in enumerate(results) if k in have]
            made = pl.pallas_call(
                functools.partial(multiply_blocks, len(carried), len(results), bases[e], len(used), h, p, gap),
                out_shape=[
                    jax.ShapeDtypeStruct((half * n, block, LANES), jnp.float32),
                    jax.ShapeDtypeStruct((n, 2 * h, 3 * p), jnp.bfloat16),
                ]
                + [jax.ShapeDtypeStruct((SENDS[i][1], block, LANES), jnp.bfloat16) for i in boxes],
                in_specs=[pl.BlockSpec(memory_space=pltpu.SMEM)] * 3
                + [pl.BlockSpec(memory_space=pltpu.VMEM)] * 2
                + [anywhere] * (len(used) + len(carried)),
                out_specs=[anywhere] * len(results),
                input_output_aliases={5 + len(used) + at: i for at, (_, i) in enumerate(carried)},
                scratch_shapes=[
                    pltpu.VMEM((2 * h, 3 * p), jnp.bfloat16),
                    pltpu.VMEM((2, 2 * h, 3 * p), jnp.bfloat16),
                    pltpu.VMEM((2, gap + h, 3 * p), jnp.bfloat16),
                    pltpu.VMEM((2, block, LANES), jnp.float32),
                    pltpu.VMEM((2, block, LANES), jnp.bfloat16),
                    pltpu.SemaphoreType.DMA,
                    pltpu.SemaphoreType.DMA((2,)),
                    pltpu.SemaphoreType.DMA,
                    pltpu.SemaphoreType.DMA((2,)),
                    pltpu.SemaphoreType.DMA((2,)),
                    pltpu.SemaphoreType.DMA((2,)),
                ],
                compiler_params=pltpu.CompilerParams(vmem_limit_bytes=64 << 20),
                cost_estimate=pl.CostEstimate(flops=1 << 20, bytes_accessed=1 << 16, transcendentals=0),
                name=f"blocks_{e}",
            )(have["line"], tile_map, group_gain, weight, group, *used, *(have[k] for k, _ in carried))
            have.update(zip(results, made))

        def exchange(i):
            ids = [((r * n + j) * 2 + y, (r * n + j) * 2 + 1 - y) for r, j, y in senders[i]]
            with jax.named_scope(f"move_sums{i}"):
                have[f"got{i}"] = lax.ppermute(have[f"sent{i}"], ("row", "col", "panel"), ids)

        move("c0", "x0", "b", "a")
        fence("own", "a", "x0", "c0", "line")
        move("xa", "ca", "d0")
        fence("b")
        choose("z", "own", "b")
        fence("b", "z", "xa", "ca", "d0")
        move("t", "xb", "cb")
        fence("cb")
        blocks(0)
        fence("sums", "sent0", "xb")
        exchange(0)
        blocks(1)
        fence("sums", "sent1", "got0", "t")
        move("e", "xt", "ct", "da", "db")
        fence("da", "db")
        blocks(2)
        fence("sums", "sent1", "ct")
        exchange(1)
        blocks(3)
        fence("sums", "sent2", "got1", "xt", "e")
        exchange(2)
        move("dt")
        blocks(4)
        fence("dt", "sums", "sent3")
        exchange(3)
        blocks(5)
        fence("sums", "sent4", "got2", "got3")
        exchange(4)
        blocks(6)
        got = [have[f"got{i}"] for i in range(len(SENDS))]
        return pl.pallas_call(
            functools.partial(add_up, final, n, h),
            out_shape=jax.ShapeDtypeStruct((half * h, 2, n * h), jnp.float32),
            in_specs=[pl.BlockSpec(memory_space=pltpu.SMEM)] + [anywhere] * (1 + len(got)),
            out_specs=anywhere,
            scratch_shapes=[
                pltpu.VMEM((half * n, block, LANES), jnp.float32),
                pltpu.VMEM((half * n, block, LANES), jnp.bfloat16),
                pltpu.VMEM((h, n * h), jnp.float32),
                pltpu.VMEM((h, n * h), jnp.float32),
                pltpu.VMEM((half, 2 * h * n * h // LANES + 8, LANES), jnp.float32),
                pltpu.SemaphoreType.DMA((half * n,)),
                pltpu.SemaphoreType.DMA((half * n,)),
                pltpu.SemaphoreType.DMA((half,)),
            ],
            compiler_params=pltpu.CompilerParams(vmem_limit_bytes=64 << 20),
            name="add_up",
        )(have["line"], have["sums"], *got)

    return local


def contract(left_side, right_side):
    return lax.dot_general(
        left_side, right_side, (((1,), (1,)), ((), ())), preferred_element_type=jnp.float32
    )


def plain(velocity, panel_weight, panel_group, tile_map, group_gain):
    row_index, col_index = lax.axis_index("row"), lax.axis_index("col")
    rows_block = lax.all_gather(velocity, "col", axis=0, tiled=True)
    kept = jnp.where(row_index == col_index, rows_block, 0).astype(rows_block.dtype)
    cols_block = lax.psum(kept, "row")
    gains = lax.dynamic_index_in_dim(group_gain, tile_map[row_index, col_index], 1, keepdims=False)
    scale = panel_weight * gains[panel_group]
    weighted = (rows_block.astype(jnp.float32) * scale[None, None, :]).astype(jnp.bfloat16)
    width, depth = weighted.shape[0], 3 * weighted.shape[2]
    left = weighted.reshape(width, 2 * depth)
    right = cols_block.reshape(width, 2 * depth)
    sign = jnp.where(row_index <= col_index, jnp.float32(1.0), jnp.float32(-1.0))
    real = contract(left[:, :depth], right[:, :depth]) + sign * contract(left[:, depth:], right[:, depth:])
    imag = contract(left[:, depth:], right[:, :depth]) - sign * contract(left[:, :depth], right[:, depth:])
    return lax.psum_scatter(jnp.stack((real, imag), axis=1), "panel", scatter_dimension=0, tiled=True)


def solution(mesh):
    n, panels = mesh.shape["col"], mesh.shape["panel"]

    def whole(velocity, panel_weight, panel_group, tile_map, group_gain):
        h = velocity.shape[0] // (n * n)
        p = velocity.shape[2] // panels
        fits = (
            mesh.shape["row"] == n
            and n == 4
            and panels == 2
            and h % 32 == 0
            and (h % LANES) * 4 == LANES
            and (n * h) % LANES == 0
            and p % LANES == 0
        )
        return jax.shard_map(
            tiled(mesh, h, p) if fits else plain,
            mesh=mesh,
            in_specs=(P(("row", "col"), None, "panel"), P("panel"), P("panel"), P(), P()),
            out_specs=P(("row", "panel"), None, "col"),
            check_vma=False,
        )(velocity, panel_weight, panel_group, tile_map, group_gain)

    return whole
```

```python
import functools

import jax
import jax.numpy as jnp
import numpy as np
from jax import lax
from jax.experimental import pallas as pl
from jax.experimental.pallas import tpu as pltpu
from jax.sharding import PartitionSpec as P

LANES = 128
KNOWN = 32
ARRIVALS = (
    (("own", "a", "b", "x0", "c0", "ca", "cb", "d0", "xa"), 5),
    (("xb",), 6),
    (("t", "da", "db"), 3),
    (("ct",), 5),
    (("e", "xt"), 2),
    (("dt",), 3),
    ((), 16),
)
SENDS = ((0, 3), (2, 2), (3, 2), (4, 2), (5, 3))


def route(n):
    devices = [(r, j) for r in range(n) for j in range(n)]
    holds = {"own": {d: d[1] for d in devices}}
    pairs, source = {}, {}

    def add(name, operand, moves):
        pairs[name], source[name] = moves, operand
        holds[name] = {t: holds[operand][f] for f, t in moves}

    ends = [(r, j) for r, j in devices if j in (0, n - 1)]
    inner = [d for d in devices if d not in ends]
    early = [(r, j) for r, j in ends if (r + j) % 2 == 0]
    add("a", "own", [((r, j ^ 1), (r, j)) for r, j in devices])
    add("b", "own", [((r, j ^ 3), (r, j)) for r, j in inner + early])
    holds["z"] = {(r, j): j ^ 3 if (r, j) in inner else j for r, j in devices}
    add("t", "z", [((r, j ^ (1 if (r, j) in ends else 2)), (r, j)) for r, j in devices])
    del holds["z"]
    add("e", "t", [((r, j ^ 1), (r, j)) for r, j in ends if (r, j) not in early])
    rows = {d: {} for d in devices}
    cols = {d: {} for d in devices}
    for name, held in holds.items():
        for device, plane in held.items():
            assert plane not in rows[device]
            rows[device][plane] = name
    for e, name in (("0", "own"), ("a", "a"), ("b", "b"), ("t", "t")):
        for v, kind in ((0, ""), (2, "x"), (1, "c"), (3, "d")):
            parent = 2 if v == 3 else 0
            if v:
                pairs[kind + e] = [((c ^ parent, c), (c ^ v, c)) for c in range(n)]
                source[kind + e] = "x" + e if parent else name
            for c in range(n):
                cols[c ^ v, c][holds[name][c, c]] = kind + e if v else name
    assert all(len(x) == n for d in devices for x in (rows[d], cols[d]))
    return pairs, source, rows, cols


def share_out(n, rows, cols):
    half = n // 2
    event = {name: e for e, (names, _) in enumerate(ARRIVALS) for name in names}
    window = [min((i for i, x in enumerate(SENDS) if x[0] >= e), default=None) for e in range(len(ARRIVALS))]
    tasks, senders, arrives = {}, [[] for _ in SENDS], {}

    def attempt(blocks, chosen):
        wait, plan = list(blocks), []
        room = [x[1] if i in chosen else 0 for i, x in enumerate(SENDS)]
        for e, (_, most) in enumerate(ARRIVALS):
            i = window[e]
            now = [b for b in wait if b[0] <= e]
            leave = [] if i is None else [b for b in now if not b[1]][:min(most, room[i])]
            if leave:
                room[i] -= len(leave)
            stay = [b for b in now if b[1]][:most - len(leave)]
            for b in leave + stay:
                wait.remove(b)
                plan.append((e, i if b in leave else None, b[2], b[3]))
        return None if wait else plan

    for r in range(n):
        for j in range(n):
            for y in range(2):
                blocks = sorted(
                    (max(event[rows[r, j][kr]], event[cols[r, j][kc]]), kr // half == y, kr, kc)
                    for kr in range(n)
                    for kc in range(n)
                )
                best = None
                for mask in range(1 << len(SENDS)):
                    chosen = [i for i in range(len(SENDS)) if mask >> i & 1]
                    plan = attempt(blocks, chosen)
                    if plan is None:
                        continue
                    cost = sum(SENDS[i][1] * i**2 for i in chosen), sum(e * e for e, _, _, _ in plan)
                    if best is None or cost < best[0]:
                        best = cost, plan
                used = {}
                for e, i, kr, kc in best[1]:
                    if i is None:
                        place = (kr - y * half) * n + kc
                    else:
                        place = used[i] = used.get(i, -1) + 1
                        arrives[r, j, 1 - y, kr, kc] = i, place
                    tasks.setdefault((r, j, y, e), []).append((kr, kc, int(i is not None), place))
                for i in used:
                    senders[i].append((r, j, y))
    return tasks, senders, arrives


def rate(w_ref, group_ref, gain_ref, region):
    groups = group_ref[...]
    gain = jnp.zeros(groups.shape, jnp.float32)
    for g in range(gain_ref.shape[0]):
        gain = gain + jnp.where(groups == g, gain_ref[g, region], jnp.float32(0.0))
    return w_ref[...] * gain


def fetch(index, sources, target, sem, h, p, gap):
    for i, source in enumerate(sources):

        @pl.when(index == i)
        def _():
            for c in range(6):
                pltpu.make_async_copy(
                    source.at[c], target.at[pl.ds((c // 3) * gap, h), pl.ds((c % 3) * p, p)], sem(c % 3)
                ).start()


def landed(sources, target, sem, h, p, gap, parts=range(6)):
    for c in parts:
        pltpu.make_async_copy(
            sources[0].at[c], target.at[pl.ds((c // 3) * gap, h), pl.ds((c % 3) * p, p)], sem
        ).wait()


def pack(stage, real, imag, h):
    tail, quarter = h % LANES, h // 2
    full = h // LANES
    for part, value in ((0, real), (1, imag)):
        for k in range(full):
            stage[pl.ds((part * full + k) * h, h), :] = value[:, k * LANES:(k + 1) * LANES].astype(stage.dtype)
        for fold in range(2):
            lane = (2 * fold + part) * tail
            stage[pl.ds(2 * full * h, quarter), lane:lane + tail] = value[
                fold * quarter:(fold + 1) * quarter, full * LANES:
            ].astype(stage.dtype)


def pick(second, first_ref, second_ref, out, held, sem):
    for k, source in enumerate((first_ref, second_ref)):

        @pl.when(second[0] == k)
        def _():
            pltpu.make_async_copy(source, held, sem).start()

    pltpu.make_async_copy(first_ref, held, sem).wait()
    copy = pltpu.make_async_copy(held, out, sem)
    copy.start()
    copy.wait()


def multiply_blocks(passed, results, base, sources, h, p, gap, table, tile_map, gain_ref, w_ref, group_ref, *refs):
    srcs = refs[:sources]
    refs = refs[sources + passed:]
    own, weighed, out = refs[0], refs[1], refs[results - 1]
    raw, left, right, stage_own, stage_out, raw_sem, l_sem, w_sem, r_sem, own_sem, out_sem = refs[results:]
    count = table[base]
    sign = table[2].astype(jnp.float32)
    scale = rate(w_ref, group_ref, gain_ref, tile_map[table[0], table[1]])

    def entry(t):
        code = table[base + 1 + t]
        return code & 63, (code >> 6) & 63, (code >> 12) & 15, (code >> 16) & 255, code >> 24

    def stored(stage, target, sem, slot, place):
        return pltpu.make_async_copy(stage.at[slot], target.at[place], sem.at[slot])

    def store(stage, target, sem, done, place, real, imag):
        slot = lax.rem(done, 2)

        @pl.when(done > 1)
        def _():
            stored(stage, target, sem, slot, 0).wait()

        pack(stage.at[slot], real, imag, h)
        stored(stage, target, sem, slot, place).start()

    def settle(stage, target, sem, done):
        for back in (1, 2):

            @pl.when(done >= back)
            def _():
                stored(stage, target, sem, lax.rem(done - back, 2), 0).wait()

    def known(slot, plane):
        return pltpu.make_async_copy(weighed.at[plane], left.at[slot], l_sem.at[slot])

    def kept(slot, plane):
        return pltpu.make_async_copy(left.at[slot], weighed.at[plane], w_sem)

    def ask_row(t, slot):
        row, plane = entry(t)[0], entry(t)[4]
        fetch(row, srcs, raw, lambda part: raw_sem.at[part], h, p, h)

        @pl.when(row >= KNOWN)
        def _():
            known(slot, plane).start()

    def ask_column(t):
        fetch(entry(t)[1], srcs, right.at[lax.rem(t, 2)], lambda _: r_sem.at[lax.rem(t, 2)], h, p, gap)

    @pl.when(count > 0)
    def _():
        ask_row(0, 0)
        ask_column(0)

    def task(t, carry):
        before, side, owns, outs = carry
        row, _, kind, place, plane = entry(t)
        slot = lax.rem(t, 2)
        changed = plane != before
        side = jnp.where(changed, 1 - side, side)
        fresh = jnp.logical_and(changed, row < KNOWN)

        @pl.when(jnp.logical_and(changed, row >= KNOWN))
        def _():
            known(side, plane).wait()

        @pl.when(fresh)
        def _():
            for c in range(3):
                landed(srcs, raw, raw_sem.at[c], h, p, h, (c, c + 3))
                part = raw[:, c * p:(c + 1) * p].astype(jnp.float32)
                left[side, :, c * p:(c + 1) * p] = (part * scale).astype(jnp.bfloat16)
            kept(side, plane).start()

        @pl.when(t + 1 < count)
        def _():
            ask_column(t + 1)

            @pl.when(entry(t + 1)[4] != plane)
            def _():
                ask_row(t + 1, 1 - side)

        landed(srcs, right.at[slot], r_sem.at[slot], h, p, gap)
        product = lax.dot_general(
            left[side], right[slot], (((1,), (1,)), ((), ())), preferred_element_type=jnp.float32
        )
        real = product[:h, :h] + sign * product[h:, gap:gap + h]
        imag = product[h:, :h] - sign * product[:h, gap:gap + h]

        @pl.when(fresh)
        def _():
            kept(side, plane).wait()

        @pl.when(kind == 0)
        def _():
            store(stage_own, own, own_sem, owns, place, real, imag)

        if results > 2:

            @pl.when(kind == 1)
            def _():
                store(stage_out, out, out_sem, outs, place, real, imag)

        return plane, side, owns + (kind == 0).astype(jnp.int32), outs + (kind == 1).astype(jnp.int32)

    zero = jnp.int32(0)
    _, _, owns, outs = lax.fori_loop(0, count, task, (zero - 1, zero + 1, zero, zero))
    settle(stage_own, own, own_sem, owns)
    if results > 2:
        settle(stage_out, out, out_sem, outs)


def add_up(base, n, h, table, own, *refs):
    recvs = refs[:len(SENDS)]
    out, mine, theirs, real, imag, image, m_sem, t_sem, o_sem = refs[len(SENDS):]
    blocks = (n // 2) * n
    full, tail, quarter = h // LANES, h % LANES, h // 2
    wide = n * h // LANES

    def written(chunk, k):
        return pltpu.make_async_copy(
            image.at[chunk, pl.ds(2 * k * h, 2 * h)].reshape(h, 2, LANES),
            out.at[pl.ds(chunk * h, h), :, pl.ds(k * LANES, LANES)],
            o_sem.at[chunk],
        )

    for b in range(blocks):
        pltpu.make_async_copy(own.at[b], mine.at[b], m_sem.at[b]).start()
        code = table[base + b]
        for k, recv in enumerate(recvs):

            @pl.when((code & 15) == k)
            def _():
                pltpu.make_async_copy(recv.at[code >> 4], theirs.at[b], t_sem.at[b]).start()

    for b in range(blocks):
        chunk, kc = b // n, b % n
        pltpu.make_async_copy(own.at[0], mine.at[b], m_sem.at[b]).wait()
        pltpu.make_async_copy(recvs[0].at[0], theirs.at[b], t_sem.at[b]).wait()
        for part, line in ((0, real), (1, imag)):
            for k in range(full):
                at = pl.ds((part * full + k) * h, h)
                line[:, kc * h + k * LANES:kc * h + (k + 1) * LANES] = mine[b, at, :] + theirs[
                    b, at, :
                ].astype(jnp.float32)
            at = pl.ds(2 * full * h, quarter)
            rest = mine[b, at, :] + theirs[b, at, :].astype(jnp.float32)
            for fold in range(2):
                lane = (2 * fold + part) * tail
                line[
                    fold * quarter:(fold + 1) * quarter, kc * h + full * LANES:(kc + 1) * h
                ] = rest[:, lane:lane + tail]
        first, last = kc * h // LANES, (kc + 1) * h // LANES
        for k in range(first, last):
            for part, line in ((0, real), (1, imag)):
                image[chunk, pl.ds(2 * k * h + part, h, stride=2), :] = line[:, k * LANES:(k + 1) * LANES]
            written(chunk, k).start()
    for chunk in range(n // 2):
        for k in range(wide):
            written(chunk, k).wait()


def tiled(mesh, h, p):
    n = mesh.shape["col"]
    half = n // 2
    pairs, source, rows, cols = route(n)
    tasks, senders, arrives = share_out(n, rows, cols)
    gap = -(-h // LANES) * LANES
    block = 2 * h * h // LANES
    events = range(len(ARRIVALS))

    names = {e: set() for e in events}
    met = {}
    for (r, j, y, e), items in tasks.items():
        for kr, _, _, _ in items:
            met[r, j, y, kr] = min(e, met.get((r, j, y, kr), e))
    for (r, j, y, e), items in tasks.items():
        for kr, kc, _, _ in items:
            names[e] |= {cols[r, j][kc]} | ({rows[r, j][kr]} if met[r, j, y, kr] == e else set())
    names = {e: sorted(v) for e, v in names.items()}
    bases, size = {}, 3
    for e in events:
        bases[e] = size
        size += 1 + max(len(v) for k, v in tasks.items() if k[3] == e)
    final = size
    size += half * n
    table = np.zeros((n, n, 2, size), np.int32)
    for r in range(n):
        for j in range(n):
            for y in range(2):
                line = table[r, j, y]
                line[:3] = r, j, 1 if r <= j else -1
                for e in events:
                    items = tasks.get((r, j, y, e), [])
                    leaving = {i[0]: -sum(x[2] for x in items if x[0] == i[0]) for i in items}
                    items = sorted(items, key=lambda i: (leaving[i[0]], i[0], -i[2], i[3]))
                    line[bases[e]] = len(items)
                    for t, (kr, kc, kind, place) in enumerate(items):
                        row = names[e].index(rows[r, j][kr]) if met[r, j, y, kr] == e else KNOWN
                        code = row | names[e].index(cols[r, j][kc]) << 6 | kind << 12 | place << 16 | kr << 24
                        line[bases[e] + 1 + t] = code
                for i in range(half):
                    for kc in range(n):
                        index, place = arrives[r, j, y, y * half + i, kc]
                        line[final + i * n + kc] = index | place << 4

    def local(velocity, panel_weight, panel_group, tile_map, group_gain):
        here = lax.axis_index("row"), lax.axis_index("col"), lax.axis_index("panel")
        line = lax.dynamic_slice(jnp.asarray(table), (*here, 0), (1, 1, 1, size)).reshape(size)
        weight, group = panel_weight[None, :], panel_group[None, :]
        have = {"own": jnp.transpose(velocity, (1, 0, 2)), "line": line}
        anywhere = pl.BlockSpec(memory_space=pl.ANY)

        def move(*given):
            for name in given:
                with jax.named_scope("move_" + name):
                    ids = [(a[0] * n + a[1], b[0] * n + b[1]) for a, b in pairs[name]]
                    have[name] = lax.ppermute(have[source[name]], ("row", "col"), ids)

        def choose(name, first, second):
            inner = jnp.logical_and(here[1] > 0, here[1] < n - 1).astype(jnp.int32)[None]
            have[name] = pl.pallas_call(
                pick,
                out_shape=jax.ShapeDtypeStruct((6, h, p), jnp.bfloat16),
                in_specs=[pl.BlockSpec(memory_space=pltpu.SMEM)] + [anywhere] * 2,
                out_specs=anywhere,
                scratch_shapes=[pltpu.VMEM((6, h, p), jnp.bfloat16), pltpu.SemaphoreType.DMA],
                compiler_params=pltpu.CompilerParams(vmem_limit_bytes=64 << 20),
                cost_estimate=pl.CostEstimate(flops=1 << 10, bytes_accessed=1 << 10, transcendentals=0),
                name="pick",
            )(inner, have[first], have[second])

        def fence(*wanted):
            keys = list(dict.fromkeys(wanted))
            have.update(zip(keys, lax.optimization_barrier(tuple(have[k] for k in keys))))

        def blocks(e):
            boxes = [i for i, x in enumerate(SENDS) if x[0] >= e][:1]
            results = ["sums", "weighed"] + [f"sent{i}" for i in boxes]
            used = [have[k] for k in names[e]]
            carried = [(k, i) for i, k in enumerate(results) if k in have]
            made = pl.pallas_call(
                functools.partial(multiply_blocks, len(carried), len(results), bases[e], len(used), h, p, gap),
                out_shape=[
                    jax.ShapeDtypeStruct((half * n, block, LANES), jnp.float32),
                    jax.ShapeDtypeStruct((n, 2 * h, 3 * p), jnp.bfloat16),
                ]
                + [jax.ShapeDtypeStruct((SENDS[i][1], block, LANES), jnp.bfloat16) for i in boxes],
                in_specs=[pl.BlockSpec(memory_space=pltpu.SMEM)] * 3
                + [pl.BlockSpec(memory_space=pltpu.VMEM)] * 2
                + [anywhere] * (len(used) + len(carried)),
                out_specs=[anywhere] * len(results),
                input_output_aliases={5 + len(used) + at: i for at, (_, i) in enumerate(carried)},
                scratch_shapes=[
                    pltpu.VMEM((2 * h, 3 * p), jnp.bfloat16),
                    pltpu.VMEM((2, 2 * h, 3 * p), jnp.bfloat16),
                    pltpu.VMEM((2, gap + h, 3 * p), jnp.bfloat16),
                    pltpu.VMEM((2, block, LANES), jnp.float32),
                    pltpu.VMEM((2, block, LANES), jnp.bfloat16),
                    pltpu.SemaphoreType.DMA((3,)),
                    pltpu.SemaphoreType.DMA((2,)),
                    pltpu.SemaphoreType.DMA,
                    pltpu.SemaphoreType.DMA((2,)),
                    pltpu.SemaphoreType.DMA((2,)),
                    pltpu.SemaphoreType.DMA((2,)),
                ],
                compiler_params=pltpu.CompilerParams(vmem_limit_bytes=64 << 20),
                cost_estimate=pl.CostEstimate(flops=1 << 20, bytes_accessed=1 << 16, transcendentals=0),
                name=f"blocks_{e}",
            )(have["line"], tile_map, group_gain, weight, group, *used, *(have[k] for k, _ in carried))
            have.update(zip(results, made))

        def exchange(i):
            ids = [((r * n + j) * 2 + y, (r * n + j) * 2 + 1 - y) for r, j, y in senders[i]]
            with jax.named_scope(f"move_sums{i}"):
                have[f"got{i}"] = lax.ppermute(have[f"sent{i}"], ("row", "col", "panel"), ids)

        move("c0", "x0", "b", "a")
        fence("own", "a", "x0", "c0", "line")
        move("xa", "ca", "d0")
        fence("b")
        choose("z", "own", "b")
        fence("b", "z", "xa", "ca", "d0")
        move("t", "xb", "cb")
        fence("cb")
        blocks(0)
        fence("sums", "sent0", "xb")
        exchange(0)
        blocks(1)
        fence("sums", "sent1", "got0", "t")
        move("e", "xt", "ct", "da", "db")
        fence("da", "db")
        blocks(2)
        fence("sums", "sent1", "ct")
        exchange(1)
        blocks(3)
        fence("sums", "sent2", "got1", "xt", "e")
        exchange(2)
        move("dt")
        blocks(4)
        fence("dt", "sums", "sent3")
        exchange(3)
        blocks(5)
        fence("sums", "sent4", "got2", "got3")
        exchange(4)
        blocks(6)
        got = [have[f"got{i}"] for i in range(len(SENDS))]
        return pl.pallas_call(
            functools.partial(add_up, final, n, h),
            out_shape=jax.ShapeDtypeStruct((half * h, 2, n * h), jnp.float32),
            in_specs=[pl.BlockSpec(memory_space=pltpu.SMEM)] + [anywhere] * (1 + len(got)),
            out_specs=anywhere,
            scratch_shapes=[
                pltpu.VMEM((half * n, block, LANES), jnp.float32),
                pltpu.VMEM((half * n, block, LANES), jnp.bfloat16),
                pltpu.VMEM((h, n * h), jnp.float32),
                pltpu.VMEM((h, n * h), jnp.float32),
                pltpu.VMEM((half, 2 * h * n * h // LANES + 8, LANES), jnp.float32),
                pltpu.SemaphoreType.DMA((half * n,)),
                pltpu.SemaphoreType.DMA((half * n,)),
                pltpu.SemaphoreType.DMA((half,)),
            ],
            compiler_params=pltpu.CompilerParams(vmem_limit_bytes=64 << 20),
            name="add_up",
        )(have["line"], have["sums"], *got)

    return local


def contract(left_side, right_side):
    return lax.dot_general(
        left_side, right_side, (((1,), (1,)), ((), ())), preferred_element_type=jnp.float32
    )


def plain(velocity, panel_weight, panel_group, tile_map, group_gain):
    row_index, col_index = lax.axis_index("row"), lax.axis_index("col")
    rows_block = lax.all_gather(velocity, "col", axis=0, tiled=True)
    kept = jnp.where(row_index == col_index, rows_block, 0).astype(rows_block.dtype)
    cols_block = lax.psum(kept, "row")
    gains = lax.dynamic_index_in_dim(group_gain, tile_map[row_index, col_index], 1, keepdims=False)
    scale = panel_weight * gains[panel_group]
    weighted = (rows_block.astype(jnp.float32) * scale[None, None, :]).astype(jnp.bfloat16)
    width, depth = weighted.shape[0], 3 * weighted.shape[2]
    left = weighted.reshape(width, 2 * depth)
    right = cols_block.reshape(width, 2 * depth)
    sign = jnp.where(row_index <= col_index, jnp.float32(1.0), jnp.float32(-1.0))
    real = contract(left[:, :depth], right[:, :depth]) + sign * contract(left[:, depth:], right[:, depth:])
    imag = contract(left[:, depth:], right[:, :depth]) - sign * contract(left[:, :depth], right[:, depth:])
    return lax.psum_scatter(jnp.stack((real, imag), axis=1), "panel", scatter_dimension=0, tiled=True)


def solution(mesh):
    n, panels = mesh.shape["col"], mesh.shape["panel"]

    def whole(velocity, panel_weight, panel_group, tile_map, group_gain):
        h = velocity.shape[0] // (n * n)
        p = velocity.shape[2] // panels
        fits = (
            mesh.shape["row"] == n
            and n == 4
            and panels == 2
            and h % 32 == 0
            and (h % LANES) * 4 == LANES
            and (n * h) % LANES == 0
            and p % LANES == 0
        )
        return jax.shard_map(
            tiled(mesh, h, p) if fits else plain,
            mesh=mesh,
            in_specs=(P(("row", "col"), None, "panel"), P("panel"), P("panel"), P(), P()),
            out_specs=P(("row", "panel"), None, "col"),
            check_vma=False,
        )(velocity, panel_weight, panel_group, tile_map, group_gain)

    return whole
```
